32 devices in a mesh: pipe: 4 (over z), dp: 8 (over y, x, core).
Axes of the slice: x: 2, y: 2, z: 4, core: 2. Of those that a mesh axis runs over, the one named last changes fastest.
Arguments:
- fwd_latents: bfloat16 [4, 6656, 1024], P('pipe', 'dp'), may hold values from -6 to 6
- fwd_segments: int32 [4, 6656], P('pipe', 'dp'), may hold values from 0 to 3, as said below
- stash_latents: bfloat16 [4, 6656, 1024], P('pipe', 'dp'), may hold values from -6 to 6
- stash_segments: int32 [4, 6656], P('pipe', 'dp'), may hold values from 0 to 3, as said below
- upstream_grad: bfloat16 [4, 6656, 1024], P('pipe', 'dp'), may hold values from -6 to 6
- qkv_weight: bfloat16 [3, 1024, 1024], P(None, 'dp'), may hold values from -0.1875 to 0.1875
- out_weight: bfloat16 [1024, 1024], P('dp'), may hold values from -3 to 3
- mlp_weight: bfloat16 [2, 1024, 1024], P(None, 'dp'), may hold values from -0.1875 to 0.1875
- norm_gain: bfloat16 [2, 1024], P(None, 'dp'), may hold values from 0.5 to 1.5
- biases: bfloat16 [7, 1024], P(None, 'dp'), may hold values from -1.5 to 1.5
Outputs:
- latents: bfloat16 [4, 6656, 1024], P('pipe', 'dp')
- input_grad: bfloat16 [4, 6656, 1024], P('pipe', 'dp')
- qkv_grad: float32 [3, 1024, 1024], P(None, 'dp')
- out_grad: float32 [1024, 1024], P('dp')
- mlp_grad: float32 [2, 1024, 1024], P(None, 'dp')
- gain_grad: float32 [2, 1024], P(None, 'dp')
- bias_grad: float32 [7, 1024], P(None, 'dp')
- shift_grad: float32 [1024], P('dp')
The draws below stay inside these ranges and needn't reach their ends.
Inputs may be any that keep to these rules, and one draw needn't show every extreme that they name: `fwd_segments`: in each device's 832 slots of a section, ids never fall; each of 0, 1, 2 that occurs marks one image of 256, 512 or 832 slots, and 3 marks the empty slots at the end. In every section one device holds one image of 832 slots and another has empty slots. `stash_segments`: as for fwd_segments.
All inputs are finite; a program needn't handle non-finite values.
Results may differ from the reference program's by a relative error of at most 0.017.
Values may be sent and summed in bfloat16 or wider, within the bound.
No kernel may reach another device: no remote copies, remote signals or barrier semaphores. Data moves between devices by JAX's collectives and lax.ppermute only.
A program may use at most 256 MiB of HBM per device.

```python
import jax
import jax.numpy as jnp
from jax import lax

D = 1024
HEADS = 8
HEAD = 128
LONG = 832
MEDIUM = 512
SHORT = 256
TOK_DEV = 832
SECTIONS = 4
TOKENS = 6656


def segment_layout(key):
    devices = TOKENS // TOK_DEV
    pick_key, full_key = jax.random.split(key)
    pattern = jax.random.randint(pick_key, (SECTIONS, devices), 0, 8)
    full_device = jax.random.randint(full_key, (SECTIONS, 1), 0, devices)
    device_place = jnp.arange(devices)[None, :]
    pattern = jnp.where(device_place == full_device, 0, pattern)
    pattern = jnp.where(device_place == (full_device + 1) % devices, 5, pattern)
    bound_table = jnp.array([[LONG, LONG, LONG], [MEDIUM, MEDIUM + SHORT, MEDIUM + SHORT], [SHORT, 2 * SHORT, 3 * SHORT], [MEDIUM, MEDIUM, MEDIUM], [SHORT, 2 * SHORT, 2 * SHORT], [SHORT, SHORT, SHORT], [SHORT, SHORT, SHORT], [SHORT, 2 * SHORT, 2 * SHORT]], jnp.int32)
    bounds = bound_table[pattern]
    slot_index = jnp.arange(TOK_DEV)
    segment_ids = jnp.sum((slot_index[None, None, :, None] >= bounds[:, :, None, :]).astype(jnp.int32), axis=-1)
    return segment_ids.reshape(SECTIONS, TOKENS).astype(jnp.int32)


def draw_fwd_segments(key, part):
    key = jax.random.fold_in(key, 11)
    return segment_layout(key)


def draw_stash_segments(key, part):
    key = jax.random.fold_in(key, 23)
    return segment_layout(key)


def with_spikes(drawn, key, source, target, blocks, factor):
    owner, partner = [(jnp.arange(drawn.shape[position]) // (drawn.shape[position] // blocks)).reshape([-1 if axis == position else 1 for axis in range(drawn.ndim)]) for position in (source, target)]
    chosen = jax.random.permutation(key, blocks)[partner]
    strong = (owner == chosen) | (owner == (partner + blocks // 2) % blocks)
    return jnp.where(strong, factor * drawn, drawn)


def steps_of(key, extent, cuts, least, largest):
    def one(position, shards_of):
        steps = jax.random.uniform(jax.random.fold_in(jax.random.fold_in(key, 6), position), (shards_of,), jnp.float32, least / len(cuts), largest / len(cuts))
        return jnp.repeat(jnp.exp(steps), extent[position] // shards_of).reshape((-1,) + (1,) * (len(extent) - position - 1))

    gain = one(*cuts[0])
    for cut in cuts[1:]:
        gain = gain * one(*cut)
    return gain


def noise(own_key, shape, scale, limit, cuts=(), dtype=jnp.bfloat16):
    level = steps_of(own_key, shape, cuts, -0.22, 0.18) if cuts else 1.0
    values = jax.random.normal(own_key, shape, jnp.float32) * scale * level
    return jnp.minimum(jnp.maximum(values, -limit), limit).astype(dtype)


def bell_draw_with(rng, shape, deviation, limit, pieces, heavy, held_as=jnp.bfloat16):
    drawn = deviation * jax.random.normal(rng, shape, jnp.float32)
    if pieces:
        drawn = drawn * steps_of(rng, shape, pieces, -0.22, 0.18)
    return jnp.clip(with_spikes(drawn, jax.random.fold_in(rng, 3), *heavy), -limit, limit).astype(held_as)


def setup_inputs(seed: int = 0) -> dict:
    key_list = jax.random.split(jax.random.key(seed), 11)
    fwd_latents = noise(key_list[0], (SECTIONS, TOKENS, D), 1.0, 6.0, ((0, 4), (1, 8)))
    fwd_segments = draw_fwd_segments(jax.random.fold_in(key_list[10], 71), 0)
    stash_latents = bell_draw_with(key_list[2], (SECTIONS, TOKENS, D), 1.0, 6.0, ((0, 4), (1, 8)), (1, 2, 8, 2.0))
    stash_segments = draw_stash_segments(jax.random.fold_in(key_list[10], 71), 0)
    upstream_grad = noise(key_list[4], (SECTIONS, TOKENS, D), 1.0, 6.0, ((0, 4), (1, 8)))
    qkv_weight = noise(key_list[5], (3, D, D), D ** -0.5, 0.1875, ((1, 8),))
    out_weight = noise(key_list[6], (D, D), (D // SHORT) ** -0.5, 3.0, ((0, 8),))
    mlp_weight = noise(key_list[7], (2, D, D), D ** -0.5, 0.1875, ((1, 8),))
    norm_gain = jnp.clip(1.0 + 0.1 * jax.random.normal(key_list[8], (2, D), jnp.float32), 0.5, 1.5).astype(jnp.bfloat16)
    biases = noise(key_list[9], (7, D), 0.3, 1.5, ((1, 8),))
    return {"fwd_latents": fwd_latents, "fwd_segments": fwd_segments, "stash_latents": stash_latents, "stash_segments": stash_segments, "upstream_grad": upstream_grad, "qkv_weight": qkv_weight, "out_weight": out_weight, "mlp_weight": mlp_weight, "norm_gain": norm_gain, "biases": biases}


EPSILON = 1e-05

@jax.custom_vjp
def low(v):
    return lax.optimization_barrier(v.astype(jnp.bfloat16)).astype(jnp.float32)

@jax.custom_vjp
def low_back(v):
    return v

def low_keep(v):
    return (low(v), None)

def low_pass(kept, grad):
    return (grad,)

def back_keep(v):
    return (v, None)

def back_low(kept, grad):
    return (low(grad),)
low.defvjp(low_keep, low_pass)
low_back.defvjp(back_keep, back_low)

def narrow_both(value):
    return low(low_back(value))

def layer_norm(latent_rows, gain_row, shift_row):
    row_mean = lax.optimization_barrier(jnp.mean(latent_rows, axis=-1, keepdims=True))
    centred = latent_rows - row_mean
    spread = lax.optimization_barrier(jnp.mean(centred * centred, axis=-1, keepdims=True))
    return centred * lax.rsqrt(spread + EPSILON) * gain_row + shift_row

def block_forward(weights, latent_rows, segment_ids):
    qkv_w, out_w, mlp_w, gains, shifts = weights
    highest = lax.Precision.HIGHEST
    count = latent_rows.shape[0]
    normed = low(layer_norm(latent_rows, gains[0], shifts[0]))
    queries = narrow_both(jnp.dot(normed, qkv_w[0], precision=highest) + shifts[1])
    key_rows = narrow_both(jnp.dot(normed, qkv_w[1], precision=highest))
    values = narrow_both(jnp.dot(normed, qkv_w[2], precision=highest) + shifts[2])
    query_heads = queries.reshape(count, HEADS, HEAD)
    key_heads = key_rows.reshape(count, HEADS, HEAD)
    value_heads = values.reshape(count, HEADS, HEAD)
    scores = low_back(jnp.einsum('qhd,khd->hqk', query_heads, key_heads, precision=highest) * HEAD ** (-0.5))
    same_image = segment_ids[:, None] == segment_ids[None, :]
    scores = jnp.where(same_image[None], scores, -1e+30)
    probs = low(jax.nn.softmax(scores, axis=-1))
    mixed = jnp.einsum('hqk,khd->qhd', probs, value_heads, precision=highest).reshape(count, D)
    mixed = narrow_both(mixed)
    attended = latent_rows + low_back(jnp.dot(mixed, out_w, precision=highest) + shifts[3])
    normed2 = low(layer_norm(attended, gains[1], shifts[4]))
    hidden = low_back(jnp.dot(normed2, mlp_w[0], precision=highest) + shifts[5])
    active = low(jax.nn.gelu(hidden))
    return attended + low_back(jnp.dot(active, mlp_w[1], precision=highest) + shifts[6])

def reference(fwd_latents, fwd_segments, stash_latents, stash_segments, upstream_grad, qkv_weight, out_weight, mlp_weight, norm_gain, biases):
    params = (qkv_weight.astype(jnp.float32), out_weight.astype(jnp.float32), mlp_weight.astype(jnp.float32), norm_gain.astype(jnp.float32), biases.astype(jnp.float32))
    blocks = SECTIONS * (TOKENS // TOK_DEV)
    checked_block = jax.checkpoint(block_forward)

    def forward_all(weights, latent_blocks, segment_blocks):

        def one_block(paired):
            return checked_block(weights, paired[0], paired[1])
        return lax.map(one_block, (latent_blocks, segment_blocks))
    fresh_ids = fwd_segments.reshape(blocks, TOK_DEV)
    fresh_rows = fwd_latents.astype(jnp.float32).reshape(blocks, TOK_DEV, D)
    forward_out = forward_all(params, fresh_rows, fresh_ids)
    forward_out = jnp.where((fresh_ids < 3)[..., None], forward_out, 0.0).reshape(SECTIONS, TOKENS, D)
    latents = jnp.roll(forward_out, 1, axis=0).astype(jnp.bfloat16)
    stash_ids = stash_segments.reshape(blocks, TOK_DEV)
    stash_rows = stash_latents.astype(jnp.float32).reshape(blocks, TOK_DEV, D)
    cotangent = jnp.roll(upstream_grad, -1, axis=0).astype(jnp.float32).reshape(blocks, TOK_DEV, D)
    cotangent = jnp.where((stash_ids < 3)[..., None], cotangent, 0.0)
    _, pull_back = jax.vjp(lambda weights, latent_blocks: forward_all(weights, latent_blocks, stash_ids), params, stash_rows)
    weight_grads, latent_grads = pull_back(cotangent)
    input_grad = latent_grads.reshape(SECTIONS, TOKENS, D).astype(jnp.bfloat16)
    return (latents, input_grad, weight_grads[0], weight_grads[1], weight_grads[2], weight_grads[3], weight_grads[4], weight_grads[4][4])
```

```python
import functools

import jax
import jax.numpy as jnp
from jax import lax
from jax.experimental import pallas as pl
from jax.experimental.pallas import tpu as pltpu
from jax.sharding import PartitionSpec as P

HEADS = 8
HEAD = 128
EPSILON = 1e-05
SCALE = HEAD ** (-0.5)
LOG2E = 1.4426950408889634
GELU_C = 0.7978845608028654
GELU_A = 0.044715
GROUPS = 2
VMEM_LIMIT = 56 * 2**20
PARAM_ROWS = 16

F32 = jnp.float32
BF16 = jnp.bfloat16
ANY = pl.BlockSpec(memory_space=pl.ANY)
VMEM = pl.BlockSpec(memory_space=pltpu.VMEM)


def sds(shape, dtype=BF16):
    return jax.ShapeDtypeStruct(shape, dtype)


def dot_nn(a, b):
    return jnp.dot(a, b, preferred_element_type=F32)


def dot_nt(a, b):
    return lax.dot_general(a, b, (((1,), (1,)), ((), ())), preferred_element_type=F32)


def dot_tn(a, b):
    return lax.dot_general(a, b, (((0,), (0,)), ((), ())), preferred_element_type=F32)


class Mover:
    def __init__(self, sems):
        self.sems = sems
        self.used = 0
        self.open = []

    def start(self, source, target):
        copy = pltpu.make_async_copy(source, target, self.sems.at[self.used])
        self.used += 1
        copy.start()
        return copy

    def put(self, source, target):
        self.open.append(self.start(source, target))

    def finish(self):
        for copy in self.open:
            copy.wait()


def load_rows(move, pieces, target, columns=None):
    source_of = (lambda ref: ref) if columns is None else (lambda ref: ref.at[:, columns])
    if len(pieces) == 1:
        return [move.start(source_of(pieces[0]), target)]
    mine = lax.axis_index("dp")
    rows = pieces[0].shape[0] // 4
    copies = []
    for step in range(4):
        for side in range(2):
            owner = mine ^ (2 * step + side)
            source = pieces[side].at[pl.ds(step * rows, rows)]
            if columns is not None:
                source = pieces[side].at[pl.ds(step * rows, rows), columns]
            copies.append(
                move.start(source, target.at[pl.ds(pl.multiple_of(owner * rows, rows), rows)])
            )
    return copies


def store_rows(move, source, pieces, columns=None):
    if len(pieces) == 1:
        target = pieces[0] if columns is None else pieces[0].at[:, columns]
        move.put(source, target)
        return
    mine = lax.axis_index("dp")
    rows = pieces[0].shape[0] // 4
    for step in range(4):
        for side in (1, 0):
            owner = mine ^ (2 * step + side)
            target = pieces[side].at[pl.ds(step * rows, rows)]
            if columns is not None:
                target = pieces[side].at[pl.ds(step * rows, rows), columns]
            move.put(source.at[pl.ds(pl.multiple_of(owner * rows, rows), rows)], target)


def wait_all(copies):
    for copy in copies:
        copy.wait()


def tiles_of(count, size):
    return [pl.ds(start, min(size, count - start)) for start in range(0, count, size)]


def normal_rows(rows):
    centred = rows - jnp.mean(rows, axis=-1, keepdims=True)
    root = lax.rsqrt(jnp.mean(centred * centred, axis=-1, keepdims=True) + EPSILON)
    return centred * root, root


def column_sum(rows):
    return jnp.sum(rows, axis=0, keepdims=True)


def kernel_call(body, name, inputs, in_specs, outs, scratch, copies, flops):
    moved = sum(a.size * a.dtype.itemsize for a in inputs)
    moved += sum(int(jnp.dtype(o.dtype).itemsize) * functools.reduce(int.__mul__, o.shape) for o in outs)
    return pl.pallas_call(
        body,
        name=name,
        out_shape=outs,
        in_specs=in_specs,
        out_specs=[ANY] * len(outs),
        scratch_shapes=list(scratch) + [pltpu.SemaphoreType.DMA((copies,))],
        compiler_params=pltpu.CompilerParams(vmem_limit_bytes=VMEM_LIMIT),
        cost_estimate=pl.CostEstimate(flops=int(flops), bytes_accessed=int(moved), transcendentals=0),
    )(*inputs)


def ln_both(first, second, params):
    count, width = first.shape

    def body(a_ref, b_ref, p_ref, na_ref, nb_ref, a, b, na, nb, sems):
        move = Mover(sems)
        loads = [move.start(a_ref, a), move.start(b_ref, b)]
        gain = p_ref[0:1, :].astype(F32)
        shift = p_ref[2:3, :].astype(F32)
        for load, rows, held, out in ((loads[0], a, na, na_ref), (loads[1], b, nb, nb_ref)):
            load.wait()
            for part in tiles_of(count, 208):
                z, _ = normal_rows(rows[part, :].astype(F32))
                held[part, :] = (z * gain + shift).astype(BF16)
            move.put(held, out)
        move.finish()

    buf = pltpu.VMEM((count, width), BF16)
    return kernel_call(
        body, "ln_both", (first, second, params), [ANY, ANY, VMEM],
        [sds((count, width))] * 2, [buf] * 4, 4, 8 * 2 * count * width,
    )


def attention_group(normed, weight, params, ids_col, ids_row, group, keep):
    count, width = normed.shape
    heads = HEADS // GROUPS
    side = heads * HEAD
    pieces = len(weight)
    tile = count // 2

    def body(*refs):
        n_ref = refs[0]
        w_refs = refs[1 : 1 + pieces]
        p_ref, col_ref, row_ref = refs[1 + pieces : 4 + pieces]
        rest = refs[4 + pieces :]
        if keep:
            q_out, k_out, v_out, o_out, e_out, l_out = rest[:6]
            normed_v, w_v, q, k, v, o, e_all, inv, sems = rest[6:]
        else:
            o_out = rest[0]
            normed_v, w_v, q, k, v, o, sems = rest[1:]
        move = Mover(sems)
        loads = [move.start(n_ref, normed_v)] + load_rows(move, w_refs, w_v)
        at = group * side
        q_shift = p_ref[3:4, at : at + side].astype(F32)
        v_shift = p_ref[4:5, at : at + side].astype(F32)
        wait_all(loads)
        for part in tiles_of(count, tile):
            projected = dot_nn(normed_v[part, :], w_v[...])
            q[part, :] = (projected[:, :side] + q_shift).astype(BF16)
            k[part, :] = projected[:, side : 2 * side].astype(BF16)
            v[part, :] = (projected[:, 2 * side :] + v_shift).astype(BF16)
        if keep:
            move.put(q, q_out)
            move.put(k, k_out)
            move.put(v, v_out)
        for head in range(heads):
            lanes = pl.ds(head * HEAD, HEAD)
            key_rows = k[:, lanes]
            value_rows = v[:, lanes]
            wide = jnp.concatenate([value_rows, jnp.ones_like(value_rows)], axis=1)
            for part in tiles_of(count, tile):
                scores = dot_nt(q[part, lanes], key_rows)
                scores = jnp.where(col_ref[part, 0:1] == row_ref[...], scores, -1e30)
                top = jnp.max(scores, axis=1, keepdims=True)
                e = jnp.exp2(scores * (SCALE * LOG2E) - top * (SCALE * LOG2E)).astype(BF16)
                if keep:
                    e_all[head, part, :] = e
                both = dot_nn(e, wide)
                inverse = 1.0 / both[:, HEAD:]
                if keep:
                    inv[part, lanes] = inverse
                o[part, lanes] = (both[:, :HEAD] * inverse).astype(BF16)
            if keep:
                move.put(e_all.at[head], e_out.at[head])
        move.put(o, o_out)
        if keep:
            move.put(inv, l_out)
        move.finish()

    buf = pltpu.VMEM((count, side), BF16)
    scratch = [
        pltpu.VMEM((count, width), BF16),
        pltpu.VMEM((width, 3 * side), BF16),
        buf, buf, buf, buf,
    ]
    outs = [sds((count, side))]
    if keep:
        scratch += [pltpu.VMEM((heads, count, count), BF16), pltpu.VMEM((count, side), F32)]
        outs = [sds((count, side))] * 4 + [sds((heads, count, count)), sds((count, side), F32)]
    flops = 2 * count * width * 3 * side + 8 * heads * count * count * HEAD
    return kernel_call(
        body, f"attention_{'stash' if keep else 'fwd'}_{group}",
        (normed, *weight, params, ids_col, ids_row),
        [ANY] * (1 + pieces) + [VMEM] * 3, outs, scratch, 9 + heads + 7, flops,
    )


def gelu_parts(hidden):
    square = hidden * hidden
    bend = jnp.tanh(GELU_C * hidden * (1.0 + GELU_A * square))
    half = 0.5 * (1.0 + bend)
    slope = half + 0.5 * hidden * (1.0 - bend * bend) * (GELU_C * (1.0 + 3.0 * GELU_A * square))
    return hidden * half, slope


def mlp_stash(latents, mixed, weight, params):
    count, width = latents.shape
    pieces = len(weight)
    split = len(mixed)
    tile = count // 4

    def body(*refs):
        x_ref = refs[0]
        m_refs = refs[1 : 1 + split]
        w_refs = refs[1 + split : 1 + split + pieces]
        p_ref = refs[1 + split + pieces]
        n_out, z_out, r_out, a_out, s_out = refs[2 + split + pieces : 7 + split + pieces]
        x, mixed_v, w, n, z_v, r_v, act, slope_v, sems = refs[7 + split + pieces :]
        move = Mover(sems)
        side = width // split
        loads = [move.start(x_ref, x)]
        for index, ref in enumerate(m_refs):
            loads.append(move.start(ref, mixed_v.at[:, pl.ds(index * side, side)]))
        loads += load_rows(move, w_refs, w)
        rows = [p_ref[i : i + 1, :].astype(F32) for i in range(9)]
        wait_all(loads)
        for part in tiles_of(count, tile):
            attended = x[part, :].astype(F32) + dot_nn(mixed_v[part, :], w[:, :width]) + rows[5]
            z, root = normal_rows(attended)
            z_v[part, :] = z.astype(BF16)
            r_v[part, :] = jnp.broadcast_to(root, (tile, 128))
            n[part, :] = (z * rows[1] + rows[6]).astype(BF16)
            hidden = dot_nn(n[part, :], w[:, width:]) + rows[7]
            active, slope = gelu_parts(hidden)
            act[part, :] = active.astype(BF16)
            slope_v[part, :] = slope.astype(BF16)
            for held, out in ((n, n_out), (z_v, z_out), (r_v, r_out), (act, a_out), (slope_v, s_out)):
                move.put(held.at[part], out.at[part])
        move.finish()

    buf = pltpu.VMEM((count, width), BF16)
    return kernel_call(
        body, "mlp_stash", (latents, *mixed, *weight, params),
        [ANY] * (1 + split + pieces) + [VMEM],
        [sds((count, width)), sds((count, width)), sds((count, 128), F32), sds((count, width)), sds((count, width))],
        [buf, buf, pltpu.VMEM((width, 2 * width), BF16), buf, buf, pltpu.VMEM((count, 128), F32), buf, buf],
        1 + split + 8 + 20, 4 * count * width * width,
    )


def mlp_fwd(latents, mixed, weight, last, params, ids_col):
    count, width = latents.shape
    pieces = len(weight)
    split = len(mixed)
    tile = count // 4

    def body(*refs):
        x_ref = refs[0]
        m_refs = refs[1 : 1 + split]
        w_refs = refs[1 + split : 1 + split + pieces]
        l_refs = refs[1 + split + pieces : 1 + split + 2 * pieces]
        p_ref, col_ref, y_out = refs[1 + split + 2 * pieces : 4 + split + 2 * pieces]
        x, mixed_v, w, w_last, y, sems = refs[4 + split + 2 * pieces :]
        move = Mover(sems)
        side = width // split
        loads = [move.start(x_ref, x)]
        for index, ref in enumerate(m_refs):
            loads.append(move.start(ref, mixed_v.at[:, pl.ds(index * side, side)]))
        loads += load_rows(move, w_refs, w)
        loads += load_rows(move, l_refs, w_last)
        rows = [p_ref[i : i + 1, :].astype(F32) for i in range(9)]
        wait_all(loads)
        for part in tiles_of(count, tile):
            attended = x[part, :].astype(F32) + dot_nn(mixed_v[part, :], w[:, :width]) + rows[5]
            z, _ = normal_rows(attended)
            normed = (z * rows[1] + rows[6]).astype(BF16)
            hidden = dot_nn(normed, w[:, width:]) + rows[7]
            active = gelu_parts(hidden)[0].astype(BF16)
            result = attended + dot_nn(active, w_last[...]) + rows[8]
            y[part, :] = jnp.where(col_ref[part, 0:1] < 3, result, 0.0).astype(BF16)
            move.put(y.at[part], y_out.at[part])
        move.finish()

    buf = pltpu.VMEM((count, width), BF16)
    return kernel_call(
        body, "mlp_fwd", (latents, *mixed, *weight, *last, params, ids_col),
        [ANY] * (1 + split + 2 * pieces) + [VMEM] * 2,
        [sds((count, width))],
        [buf, buf, pltpu.VMEM((width, 2 * width), BF16), pltpu.VMEM((width, width), BF16), buf],
        1 + split + 16 + 4, 6 * count * width * width,
    )[0]


def mlp_backward(arrived, ids_col, active, slope, normed, last, shards):
    count, width = active.shape
    pieces = len(last)
    tile = count // 2

    def body(*refs):
        g_ref, a_ref, s_ref, n_ref = refs[:4]
        w_refs = refs[4 : 4 + pieces]
        col_ref = refs[4 + pieces]
        rest = refs[5 + pieces :]
        d_out, c_out, b_out = rest[:3]
        grads = rest[3 : 3 + pieces]
        g, act, slo, n, w, dout, dhid, terms, sums, sems = rest[3 + pieces :]
        move = Mover(sems)
        load_g = move.start(g_ref, g)
        load_w = load_rows(move, w_refs, w)
        load_s = move.start(s_ref, slo)
        load_a = move.start(a_ref, act)
        load_n = move.start(n_ref, n)
        load_g.wait()
        dout[...] = jnp.where(col_ref[:, 0:1] < 3, g[...].astype(F32), 0.0).astype(BF16)
        move.put(dout, c_out)
        wait_all(load_w)
        load_s.wait()
        first = jnp.zeros((1, width), F32)
        second = jnp.zeros((1, width), F32)
        for part in tiles_of(count, tile):
            dactive = dot_nt(dout[part, :], w[...])
            held = (slo[part, :].astype(F32) * dactive).astype(BF16)
            dhid[part, :] = held
            first += column_sum(held.astype(F32))
            second += column_sum(dout[part, :].astype(F32))
        sums[0:1, :] = first
        sums[1:2, :] = second
        move.put(dhid, d_out)
        move.put(sums, b_out)
        load_n.wait()
        terms[:, :width] = dot_tn(n[...], dhid[...]).astype(BF16)
        load_a.wait()
        terms[:, width:] = dot_tn(act[...], dout[...]).astype(BF16)
        store_rows(move, terms, grads)
        move.finish()

    buf = pltpu.VMEM((count, width), BF16)
    return kernel_call(
        body, "mlp_backward", (arrived, active, slope, normed, *last, ids_col),
        [ANY] * (4 + pieces) + [VMEM],
        [sds((count, width)), sds((count, width)), sds((8, width), F32)]
        + [sds((shards, 2 * width))] * pieces,
        [buf, buf, buf, buf, pltpu.VMEM((width, width), BF16), buf, buf,
         pltpu.VMEM((width, 2 * width), BF16), pltpu.VMEM((8, width), F32)],
        4 + 8 + 3 + 8, 6 * count * width * width,
    )


def out_backward(dhidden, dout, z2, root2, mixed, weight, params, shards):
    count, width = dhidden.shape
    pieces = len(weight)
    split = len(mixed)
    tile = count // 4

    def body(*refs):
        h_ref, c_ref, z_ref, r_ref = refs[:4]
        m_refs = refs[4 : 4 + split]
        w_refs = refs[4 + split : 4 + split + pieces]
        p_ref = refs[4 + split + pieces]
        rest = refs[5 + split + pieces :]
        d_out, m_out, b_out = rest[:3]
        grads = rest[3 : 3 + pieces]
        dhid, cot, z_v, r_v, mixed_v, w, datt, dattn, dmix, terms, sums, sems = rest[3 + pieces :]
        move = Mover(sems)
        side = width // split
        loads = [move.start(h_ref, dhid)]
        loads += load_rows(move, w_refs, w)
        loads += [move.start(c_ref, cot), move.start(z_ref, z_v), move.start(r_ref, r_v)]
        late = []
        for index, ref in enumerate(m_refs):
            late.append(move.start(ref, mixed_v.at[:, pl.ds(index * side, side)]))
        gain = p_ref[1:2, :].astype(F32)
        wait_all(loads)
        totals = [jnp.zeros((1, width), F32) for _ in range(3)]
        for part in tiles_of(count, tile):
            dnormed = dot_nt(dhid[part, :], w[:, width:])
            z = z_v[part, :].astype(F32)
            totals[0] += column_sum(dnormed * z)
            totals[1] += column_sum(dnormed)
            dz = dnormed * gain
            inner = dz - jnp.mean(dz, axis=-1, keepdims=True)
            inner = inner - z * jnp.mean(dz * z, axis=-1, keepdims=True)
            dattended = cot[part, :].astype(F32) + r_v[part, 0:1] * inner
            datt[part, :] = dattended
            held = dattended.astype(BF16)
            dattn[part, :] = held
            totals[2] += column_sum(held.astype(F32))
            dmix[part, :] = dot_nt(held, w[:, :width]).astype(BF16)
            move.put(datt.at[part], d_out.at[part])
            move.put(dmix.at[part], m_out.at[part])
        for index in range(3):
            sums[index : index + 1, :] = totals[index]
        move.put(sums, b_out)
        wait_all(late)
        terms[...] = dot_tn(mixed_v[...], dattn[...]).astype(BF16)
        store_rows(move, terms, grads)
        move.finish()

    buf = pltpu.VMEM((count, width), BF16)
    return kernel_call(
        body, "out_backward", (dhidden, dout, z2, root2, *mixed, *weight, params),
        [ANY] * (4 + split + pieces) + [VMEM],
        [sds((count, width), F32), sds((count, width)), sds((8, width), F32)]
        + [sds((shards, width))] * pieces,
        [buf, buf, buf, pltpu.VMEM((count, 128), F32), buf, pltpu.VMEM((width, 2 * width), BF16),
         pltpu.VMEM((count, width), F32), buf, buf, pltpu.VMEM((width, width), BF16),
         pltpu.VMEM((8, width), F32)],
        4 + split + 8 + 8 + 1 + 8, 6 * count * width * width,
    )


def attention_backward(saved, dmixed, normed, group, shards, pieces):
    queries, key_rows, values, mixed, weights, inverse = saved
    count, width = normed.shape
    heads = HEADS // GROUPS
    side = heads * HEAD
    tile = count // 2

    def body(*refs):
        q_ref, k_ref, v_ref, o_ref, e_ref, l_ref, m_ref, n_ref = refs[:8]
        d_out, b_out = refs[8:10]
        grads = refs[10 : 10 + pieces]
        q, k, v, o, e, inv, dmix, n, dqkv, dscore, terms, sums, sems = refs[10 + pieces :]
        move = Mover(sems)
        loads = [
            move.start(m_ref.at[:, pl.ds(group * side, side)], dmix),
            move.start(l_ref, inv), move.start(o_ref, o), move.start(v_ref, v),
            move.start(k_ref, k), move.start(q_ref, q),
        ]
        load_e = [move.start(e_ref.at[head], e.at[head]) for head in range(heads)]
        load_n = move.start(n_ref, n)
        wait_all(loads)
        for head in range(heads):
            lanes = pl.ds(head * HEAD, HEAD)
            scaled = (dmix[:, lanes].astype(F32) * inv[:, lanes]).astype(BF16)
            row_sum = jnp.sum(scaled.astype(F32) * o[:, lanes].astype(F32), axis=1, keepdims=True)
            value_rows = v[:, lanes]
            head_keys = k[:, lanes]
            load_e[head].wait()
            for start in range(0, count, tile):
                part = pl.ds(start, tile)
                dprobs = dot_nt(scaled[start : start + tile], value_rows)
                held = e[head, part, :].astype(F32) * (dprobs - row_sum[start : start + tile])
                held = held.astype(BF16)
                dscore[part, :] = held
                dqkv[part, lanes] = (dot_nn(held, head_keys) * SCALE).astype(BF16)
            dqkv[:, pl.ds(side + head * HEAD, HEAD)] = (
                dot_tn(dscore[...], q[:, lanes]) * SCALE
            ).astype(BF16)
            dqkv[:, pl.ds(2 * side + head * HEAD, HEAD)] = dot_tn(e[head], scaled).astype(BF16)
        move.put(dqkv, d_out)
        sums[0:1, :] = column_sum(dqkv[:, :side].astype(F32))
        sums[1:2, :] = column_sum(dqkv[:, 2 * side :].astype(F32))
        move.put(sums, b_out)
        load_n.wait()
        terms[...] = dot_tn(n[...], dqkv[...]).astype(BF16)
        store_rows(move, terms, grads)
        move.finish()

    buf = pltpu.VMEM((count, side), BF16)
    return kernel_call(
        body, f"attention_backward_{group}",
        (queries, key_rows, values, mixed, weights, inverse, dmixed, normed),
        [ANY] * 8,
        [sds((count, 3 * side)), sds((8, side), F32)] + [sds((shards, 3 * side))] * pieces,
        [buf, buf, buf, buf, pltpu.VMEM((heads, count, count), BF16), pltpu.VMEM((count, side), F32),
         buf, pltpu.VMEM((count, width), BF16), pltpu.VMEM((count, 3 * side), BF16),
         pltpu.VMEM((count, count), BF16), pltpu.VMEM((width, 3 * side), BF16), pltpu.VMEM((8, side), F32)],
        8 + heads + 2 + 8, 2 * count * width * 3 * side + 16 * heads * count * count * HEAD,
    )


def input_backward(latents, dattended, parts, weights, params):
    count, width = latents.shape
    pieces = len(weights[0])
    groups = len(parts)
    side3 = parts[0].shape[1]
    tile = count // 4

    def body(*refs):
        x_ref, d_ref = refs[:2]
        g_refs = refs[2 : 2 + groups]
        at = 2 + groups
        w_refs = [refs[at + i * pieces : at + (i + 1) * pieces] for i in range(groups)]
        at += groups * pieces
        p_ref, y_out, b_out = refs[at : at + 3]
        x, datt, dqkv, w, y, sums, sems = refs[at + 3 :]
        move = Mover(sems)
        loads = []
        for index in range(groups):
            loads.append(move.start(g_refs[index], dqkv.at[index]))
            loads += load_rows(move, w_refs[index], w.at[index])
        loads += [move.start(x_ref, x), move.start(d_ref, datt)]
        gain = p_ref[0:1, :].astype(F32)
        wait_all(loads)
        totals = [jnp.zeros((1, width), F32) for _ in range(2)]
        for part in tiles_of(count, tile):
            dnormed = dot_nt(dqkv[0, part, :], w[0])
            for index in range(1, groups):
                dnormed += dot_nt(dqkv[index, part, :], w[index])
            z, root = normal_rows(x[part, :].astype(F32))
            totals[0] += column_sum(dnormed * z)
            totals[1] += column_sum(dnormed)
            dz = dnormed * gain
            inner = dz - jnp.mean(dz, axis=-1, keepdims=True)
            inner = inner - z * jnp.mean(dz * z, axis=-1, keepdims=True)
            y[part, :] = (datt[part, :] + root * inner).astype(BF16)
            move.put(y.at[part], y_out.at[part])
        for index in range(2):
            sums[index : index + 1, :] = totals[index]
        move.put(sums, b_out)
        move.finish()

    buf = pltpu.VMEM((count, width), BF16)
    return kernel_call(
        body, "input_backward",
        (latents, dattended, *parts, *[piece for weight in weights for piece in weight], params),
        [ANY] * (2 + groups + groups * pieces) + [VMEM],
        [sds((count, width)), sds((8, width), F32)],
        [buf, pltpu.VMEM((count, width), F32), pltpu.VMEM((groups, count, side3), BF16),
         pltpu.VMEM((groups, width, side3), BF16), buf, pltpu.VMEM((8, width), F32)],
        2 + 9 * groups + 5, 2 * count * width * side3 * groups,
    )


def swapped(value, axis, flip):
    count = lax.axis_size(axis)
    return lax.ppermute(value, axis, [(source, source ^ flip) for source in range(count)])


def shifted(value, axis, steps):
    count = lax.axis_size(axis)
    pairs = [(source, (source + steps) % count) for source in range(count)]
    return lax.ppermute(value, axis, pairs)


def after(value, *others):
    return lax.optimization_barrier((value, *others))[0]


def gather_rows(shard):
    if lax.axis_size("dp") != 8:
        return (lax.all_gather(shard, "dp", axis=0, tiled=True),), ()
    arrived = [swapped(shard, "dp", flip) for flip in (2, 4, 6)]
    side = jnp.concatenate([shard, *arrived], axis=0)
    return (side, swapped(side, "dp", 1)), tuple(arrived)


def scatter_sum(pieces):
    if lax.axis_size("dp") != 8:
        return lax.psum_scatter(pieces[0], "dp", scatter_dimension=0, tiled=True)
    mine, theirs = pieces
    other = swapped(theirs, "dp", 1)
    rows = mine.shape[0] // 4
    pair = []
    for step in range(4):
        part = slice(step * rows, (step + 1) * rows)
        pair.append((mine[part].astype(F32) + other[part].astype(F32)).astype(BF16))
    arrived = [swapped(pair[step], "dp", 2 * step) for step in (1, 2, 3)]
    total = pair[0].astype(F32)
    for value in arrived:
        total = total + value.astype(F32)
    return total.astype(BF16)


def pipe_sum(shard):
    count = lax.axis_size("pipe")
    rows = shard.shape[0] // count
    if count != 4 or rows % 16:
        return lax.psum(shard, "pipe")
    place = lax.axis_index("pipe")

    def quarter(step):
        return lax.dynamic_slice_in_dim(shard, (place + step) % count * rows, rows, axis=0)

    total = quarter(0).astype(F32)
    for value in [shifted(quarter(step), "pipe", step) for step in range(1, count)]:
        total = total + value.astype(F32)
    total = total.astype(BF16)
    result = lax.dynamic_update_slice_in_dim(jnp.zeros_like(shard), total, place * rows, axis=0)
    for step, value in [(step, shifted(total, "pipe", step)) for step in range(1, count)]:
        result = lax.dynamic_update_slice_in_dim(
            result, value, (place + count - step) % count * rows, axis=0
        )
    return result


def ordered_sum(value):
    count = lax.axis_size("pipe")
    place = lax.axis_index("pipe")
    blocks = jnp.zeros((count, *value.shape), value.dtype)
    for step in range(count):
        block = shifted(value, "pipe", step) if step else value
        blocks = lax.dynamic_update_index_in_dim(blocks, block, (place + count - step) % count, axis=0)
    total = blocks[0].astype(F32)
    for index in range(1, count):
        total = total + blocks[index].astype(F32)
    return total


def shard_major(rows):
    count = lax.axis_size("dp")
    blocks = rows.reshape(rows.shape[0], count, rows.shape[1] // count).transpose(1, 0, 2)
    if count != 8:
        return (blocks.reshape(-1, blocks.shape[2]),)
    mine = lax.axis_index("dp")

    def pick(flip):
        return lax.dynamic_index_in_dim(blocks, mine ^ flip, axis=0, keepdims=False)

    return tuple(
        jnp.concatenate([pick(2 * step + side) for step in range(4)], axis=0) for side in range(2)
    )


def gather_params(norm_gain, biases):
    width = norm_gain.shape[1]
    count = lax.axis_size("dp")
    shard = jnp.concatenate(
        [norm_gain, biases, jnp.zeros((PARAM_ROWS - 9, width), norm_gain.dtype)], axis=0
    )
    pieces, arrived = gather_rows(shard)
    if len(pieces) == 1:
        blocks = pieces[0].reshape(count, PARAM_ROWS, width)
        return blocks.transpose(1, 0, 2).reshape(PARAM_ROWS, count * width), arrived

    def body(a_ref, b_ref, out):
        mine = lax.axis_index("dp")
        for step in range(4):
            for side, ref in enumerate((a_ref, b_ref)):
                owner = mine ^ (2 * step + side)
                lanes = pl.ds(pl.multiple_of(owner * width, width), width)
                out[:, lanes] = ref[pl.ds(step * PARAM_ROWS, PARAM_ROWS), :]

    full = pl.pallas_call(
        body, name="params_in_order", out_shape=sds((PARAM_ROWS, count * width)),
        in_specs=[VMEM, VMEM], out_specs=VMEM,
    )(*pieces)
    return full, arrived


def local(
    fwd_latents,
    fwd_segments,
    stash_latents,
    stash_segments,
    upstream_grad,
    qkv_weight,
    out_weight,
    mlp_weight,
    norm_gain,
    biases,
):
    fwd_x, stash_x = fwd_latents[0], stash_latents[0]
    count, width = fwd_x.shape
    rows = qkv_weight.shape[1]
    side = width // GROUPS
    pieces = 2 if lax.axis_size("dp") == 8 else 1
    shards = width // pieces
    params, hold = gather_params(norm_gain, biases)
    fwd_row, stash_row = fwd_segments, stash_segments
    fwd_col = jnp.broadcast_to(fwd_segments[0][:, None], (count, 128))
    stash_col = jnp.broadcast_to(stash_segments[0][:, None], (count, 128))
    arrived = shifted(upstream_grad[0], "pipe", -1)

    qkv_parts = []
    for group in range(GROUPS):
        cut = qkv_weight[:, :, group * side : (group + 1) * side]
        shard = jnp.concatenate([cut[0], cut[1], cut[2]], axis=1)
        gathered, hold = gather_rows(after(shard, *hold))
        qkv_parts.append(gathered)
    middle, hold = gather_rows(
        after(jnp.concatenate([out_weight, mlp_weight[0]], axis=1), *hold)
    )
    last, hold = gather_rows(after(mlp_weight[1], *hold))

    fwd_normed, stash_normed = ln_both(fwd_x, stash_x, params)
    saved = []
    fwd_mixed = []
    for group in range(GROUPS):
        saved.append(
            attention_group(stash_normed, qkv_parts[group], params, stash_col, stash_row, group, True)
        )
        fwd_mixed += attention_group(
            fwd_normed, qkv_parts[group], params, fwd_col, fwd_row, group, False
        )
    stash_mixed = [group[3] for group in saved]
    normed2, z2, root2, active, slope = mlp_stash(stash_x, stash_mixed, middle, params)
    result = mlp_fwd(fwd_x, fwd_mixed, middle, last, params, fwd_col)
    latents = shifted(result[None], "pipe", 1)

    dhidden, dout, mlp_sums, *mlp_terms = mlp_backward(
        arrived, stash_col, active, slope, normed2, last, shards
    )
    mlp_total = pipe_sum(scatter_sum(mlp_terms))
    dattended, dmixed, out_sums, *out_terms = out_backward(
        dhidden, dout, z2, root2, stash_mixed, middle, params, shards
    )
    out_total = pipe_sum(scatter_sum(out_terms))
    dprojected, qkv_totals, qkv_sums = [], [], []
    for group in range(GROUPS):
        part, sums, *terms = attention_backward(
            saved[group], dmixed, stash_normed, group, shards, pieces
        )
        dprojected.append(part)
        qkv_sums.append(sums)
        qkv_totals.append(pipe_sum(scatter_sum(terms)))
    input_grad, in_sums = input_backward(stash_x, dattended, dprojected, qkv_parts, params)

    query_shift = jnp.concatenate([sums[0:1] for sums in qkv_sums], axis=1)
    value_shift = jnp.concatenate([sums[1:2] for sums in qkv_sums], axis=1)
    small = jnp.concatenate(
        [
            in_sums[0:1], out_sums[0:1], in_sums[1:2], query_shift, value_shift,
            out_sums[2:3], out_sums[1:2], mlp_sums[0:1], mlp_sums[1:2],
            jnp.zeros((PARAM_ROWS - 9, width), F32),
        ],
        axis=0,
    ).astype(BF16)
    small_sum = ordered_sum(scatter_sum(shard_major(small)))

    qkv_grad = jnp.stack(
        [
            jnp.concatenate([total[:, s * side : (s + 1) * side] for total in qkv_totals], axis=1)
            for s in range(3)
        ]
    ).astype(F32)
    mlp_grad = jnp.stack([mlp_total[:, :width], mlp_total[:, width:]]).astype(F32)
    return (
        latents,
        input_grad[None],
        qkv_grad,
        out_total.astype(F32),
        mlp_grad,
        small_sum[0:2],
        small_sum[2:9],
        small_sum[6],
    )


def solution(mesh):
    in_specs = (
        P("pipe", "dp", None),
        P("pipe", "dp"),
        P("pipe", "dp", None),
        P("pipe", "dp"),
        P("pipe", "dp", None),
        P(None, "dp", None),
        P("dp", None),
        P(None, "dp", None),
        P(None, "dp"),
        P(None, "dp"),
    )
    out_specs = (
        P("pipe", "dp", None),
        P("pipe", "dp", None),
        P(None, "dp", None),
        P("dp", None),
        P(None, "dp", None),
        P(None, "dp"),
        P(None, "dp"),
        P("dp"),
    )
    return jax.shard_map(local, mesh=mesh, in_specs=in_specs, out_specs=out_specs, check_vma=False)
```

```python
import functools

import jax
import jax.numpy as jnp
from jax import lax
from jax.experimental import pallas as pl
from jax.experimental.pallas import tpu as pltpu
from jax.sharding import PartitionSpec as P

HEADS = 8
HEAD = 128
EPSILON = 1e-05
SCALE = HEAD ** (-0.5)
LOG2E = 1.4426950408889634
GELU_C = 0.7978845608028654
GELU_A = 0.044715
FORWARD_GROUPS = ((0, 1), (1, 3), (4, 4))
BACKWARD_GROUPS = ((0, 3), (3, 3), (6, 2))
VMEM_LIMIT = 56 * 2**20
PARAM_ROWS = 16

F32 = jnp.float32
BF16 = jnp.bfloat16
ANY = pl.BlockSpec(memory_space=pl.ANY)
VMEM = pl.BlockSpec(memory_space=pltpu.VMEM)


def sds(shape, dtype=BF16):
    return jax.ShapeDtypeStruct(shape, dtype)


def dot_nn(a, b):
    return jnp.dot(a, b, preferred_element_type=F32)


def dot_nt(a, b):
    return lax.dot_general(a, b, (((1,), (1,)), ((), ())), preferred_element_type=F32)


def dot_tn(a, b):
    return lax.dot_general(a, b, (((0,), (0,)), ((), ())), preferred_element_type=F32)


class Mover:
    def __init__(self, sems):
        self.sems = sems
        self.used = 0
        self.open = []

    def start(self, source, target):
        copy = pltpu.make_async_copy(source, target, self.sems.at[self.used])
        self.used += 1
        copy.start()
        return copy

    def put(self, source, target):
        self.open.append(self.start(source, target))

    def finish(self):
        for copy in self.open:
            copy.wait()


def load_rows(move, pieces, target, columns=None, rows=None):
    columns = pl.ds(0, target.shape[1]) if columns is None else columns
    if len(pieces) == 1:
        return [move.start(pieces[0].at[pl.ds(0, target.shape[0]), columns], target)]
    mine = lax.axis_index("dp")
    step_rows = pieces[0].shape[0] // 4
    rows = step_rows if rows is None else rows
    copies = []
    for step in range(4):
        for side in range(2):
            owner = mine ^ (2 * step + side)
            source = pieces[side].at[pl.ds(step * step_rows, rows), columns]
            copies.append(
                move.start(source, target.at[pl.ds(pl.multiple_of(owner * rows, rows), rows)])
            )
    return copies


def load_side_by_side(move, refs, target):
    copies, place = [], 0
    for ref in refs:
        copies.append(move.start(ref, target.at[:, pl.ds(place, ref.shape[1])]))
        place += ref.shape[1]
    return copies


def store_rows(move, source, pieces, extra):
    count = lax.axis_size("dp")
    rows = source.shape[0] // count
    whole = rows + extra.shape[0]
    mine = lax.axis_index("dp")
    for index in range(count):
        if len(pieces) == 1:
            owner, target, place = index, pieces[0], index
        else:
            owner, target, place = mine ^ index, pieces[index % 2], index // 2
        start = pl.multiple_of(owner * rows, rows)
        move.put(source.at[pl.ds(start, rows)], target.at[pl.ds(place * whole, rows)])
        move.put(extra, target.at[pl.ds(place * whole + rows, extra.shape[0])])


def term_shapes(width, columns, sides):
    count = lax.axis_size("dp")
    return [sds(((width + count * PARAM_ROWS) // sides, columns))] * sides


def wait_all(copies):
    for copy in copies:
        copy.wait()


def tiles_of(count, size):
    return [pl.ds(start, min(size, count - start)) for start in range(0, count, size)]


def normal_rows(rows):
    centred = rows - jnp.mean(rows, axis=-1, keepdims=True)
    root = lax.rsqrt(jnp.mean(centred * centred, axis=-1, keepdims=True) + EPSILON)
    return centred * root, root


def column_sum(rows):
    return jnp.sum(rows, axis=0, keepdims=True)


def kernel_call(body, name, inputs, in_specs, outs, scratch, copies, flops):
    moved = sum(a.size * a.dtype.itemsize for a in inputs)
    moved += sum(int(jnp.dtype(o.dtype).itemsize) * functools.reduce(int.__mul__, o.shape) for o in outs)
    return pl.pallas_call(
        body,
        name=name,
        out_shape=outs,
        in_specs=in_specs,
        out_specs=[ANY] * len(outs),
        scratch_shapes=list(scratch) + [pltpu.SemaphoreType.DMA((copies,))],
        compiler_params=pltpu.CompilerParams(vmem_limit_bytes=VMEM_LIMIT),
        cost_estimate=pl.CostEstimate(flops=int(flops), bytes_accessed=int(moved), transcendentals=0),
    )(*inputs)


def load_params(move, pieces, rows, target):
    mine = lax.axis_index("dp")
    step_rows = pieces[0].shape[0] // 4
    width = target.shape[1] // 8
    copies = []
    for step in range(4):
        for side in range(2):
            owner = mine ^ (2 * step + side)
            copies.append(
                move.start(
                    pieces[side].at[pl.ds(step * step_rows + rows, PARAM_ROWS), pl.ds(0, width)],
                    target.at[:, pl.ds(pl.multiple_of(owner * width, width), width)],
                )
            )
    return copies


def attention_group(batches, weight, params, first_head, heads):
    count, width = batches[0][0].shape
    side = heads * HEAD
    pieces = len(weight)
    total = len(batches)
    tile = count // 2
    opening = params is None
    own_rows = width // 8 if pieces == 2 else width

    def body(*refs):
        inputs = [refs[3 * i : 3 * i + 3] for i in range(total)]
        w_refs = refs[3 * total : 3 * total + pieces]
        at = 3 * total + pieces
        if not opening:
            p_ref = refs[at]
            at += 1
        outputs = []
        for _, _, _, keep in batches:
            outputs.append(refs[at : at + (6 if keep else 1)])
            at += 6 if keep else 1
        if opening:
            normed_outs = refs[at : at + total]
            z_out, p_out = refs[at + total : at + total + 2]
            at += total + 2
        params_v, w_v, *held = refs[at:-1]
        if opening:
            z_v, *held = held
        move = Mover(refs[-1])
        if not opening:
            loads = [move.start(p_ref, params_v)]
        else:
            loads = load_params(move, w_refs, own_rows, params_v)
        scratch, batch_loads = [], []
        for index, (_, _, _, keep) in enumerate(batches):
            scratch.append(held[: 9 if keep else 7])
            held = held[9 if keep else 7 :]
            n_ref, col_ref, row_ref = inputs[index]
            normed_v, col_v, row_v = scratch[index][:3]
            batch_loads.append(move.start(n_ref, normed_v))
            if index == 0:
                w_loads = load_rows(move, w_refs, w_v, rows=own_rows)
            scratch[index] = (*scratch[index], move.start(col_ref, col_v), move.start(row_ref, row_v))
        wait_all(loads)
        if opening:
            move.put(params_v, p_out)
        at = first_head * HEAD
        q_shift = params_v[3:4, at : at + side].astype(F32)
        v_shift = params_v[4:5, at : at + side].astype(F32)
        for index, (_, _, _, keep) in enumerate(batches):
            normed_v, col_v, row_v, q, k, v, o = scratch[index][:7]
            batch_loads[index].wait()
            if opening:
                gain = params_v[0:1, :].astype(F32)
                shift = params_v[2:3, :].astype(F32)
                for part in tiles_of(count, 208):
                    z, _ = normal_rows(normed_v[part, :].astype(F32))
                    normed_v[part, :] = (z * gain + shift).astype(BF16)
                    if keep:
                        z_v[part, :] = z.astype(BF16)
                move.put(normed_v, normed_outs[index])
                if keep:
                    move.put(z_v, z_out)
            if index == 0:
                wait_all(w_loads)
            for part in tiles_of(count, tile):
                projected = dot_nn(normed_v[part, :], w_v[...])
                q[part, :] = (projected[:, :side] + q_shift).astype(BF16)
                k[part, :] = projected[:, side : 2 * side].astype(BF16)
                v[part, :] = (projected[:, 2 * side :] + v_shift).astype(BF16)
            if keep:
                q_out, k_out, v_out, o_out, e_out, l_out = outputs[index]
                e_all, inv = scratch[index][7:9]
                move.put(q, q_out)
                move.put(k, k_out)
                move.put(v, v_out)
            else:
                o_out = outputs[index][0]
            wait_all(scratch[index][-2:])
            for head in range(heads):
                lanes = pl.ds(head * HEAD, HEAD)
                key_rows = k[:, lanes]
                value_rows = v[:, lanes]
                wide = jnp.concatenate([value_rows, jnp.ones_like(value_rows)], axis=1)
                for part in tiles_of(count, tile):
                    scores = dot_nt(q[part, lanes], key_rows)
                    scores = jnp.where(col_v[part, 0:1] == row_v[...], scores, -1e30)
                    top = jnp.max(scores, axis=1, keepdims=True)
                    e = jnp.exp2(scores * (SCALE * LOG2E) - top * (SCALE * LOG2E)).astype(BF16)
                    if keep:
                        e_all[head, part, :] = e
                    both = dot_nn(e, wide)
                    inverse = 1.0 / both[:, HEAD:]
                    if keep:
                        inv[part, lanes] = inverse
                    o[part, lanes] = (both[:, :HEAD] * inverse).astype(BF16)
                if keep:
                    move.put(e_all.at[head], e_out.at[head])
            move.put(o, o_out)
            if keep:
                move.put(inv, l_out)
        move.finish()

    buf = pltpu.VMEM((count, side), BF16)
    scratch = [pltpu.VMEM((PARAM_ROWS, width), BF16), pltpu.VMEM((width, 3 * side), BF16)]
    scratch += [pltpu.VMEM((count, width), BF16)] if opening else []
    outs, inputs = [], []
    for normed, ids_col, ids_row, keep in batches:
        inputs += [normed, ids_col, ids_row]
        scratch += [
            pltpu.VMEM((count, width), BF16), pltpu.VMEM(ids_col.shape, jnp.int32),
            pltpu.VMEM(ids_row.shape, jnp.int32), buf, buf, buf, buf,
        ]
        outs += [sds((count, side))]
        if keep:
            scratch += [pltpu.VMEM((heads, count, count), BF16), pltpu.VMEM((count, side), F32)]
            outs += [sds((count, side))] * 3 + [sds((heads, count, count)), sds((count, side), F32)]
    if opening:
        outs += [sds((count, width))] * (total + 1) + [sds((PARAM_ROWS, width))]
    flops = total * (2 * count * width * 3 * side + 8 * heads * count * count * HEAD)
    result = kernel_call(
        body, f"attention_{'_'.join('stash' if b[3] else 'fwd' for b in batches)}_{first_head}",
        (*inputs, *weight, *([] if opening else [params])),
        [ANY] * (3 * total + pieces + (0 if opening else 1)), outs, scratch,
        19 + total * (4 + 5 + heads), flops,
    )
    split = []
    for _, _, _, keep in batches:
        split.append(result[: 6 if keep else 1])
        result = result[6 if keep else 1 :]
    return split, result


def gelu_parts(hidden):
    square = hidden * hidden
    bend = jnp.tanh(GELU_C * hidden * (1.0 + GELU_A * square))
    half = 0.5 * (1.0 + bend)
    slope = half + 0.5 * hidden * (1.0 - bend * bend) * (GELU_C * (1.0 + 3.0 * GELU_A * square))
    return hidden * half, slope


def mlp_fwd(latents, mixed, weight, last, params, ids_col, cuts):
    count, width = latents.shape
    pieces = len(weight)
    split = len(mixed)
    tile = count // 4

    def body(*refs):
        x_ref = refs[0]
        m_refs = refs[1 : 1 + split]
        w_refs = refs[1 + split : 1 + split + pieces]
        l_refs = refs[1 + split + pieces : 1 + split + 2 * pieces]
        p_ref, col_ref = refs[1 + split + 2 * pieces : 3 + split + 2 * pieces]
        y_outs = refs[3 + split + 2 * pieces : 3 + split + 2 * pieces + len(cuts)]
        x, mixed_v, w, w_last, p, col, rest, n, y, sems = refs[3 + split + 2 * pieces + len(cuts) :]
        move = Mover(sems)
        loads = [move.start(p_ref, p), move.start(x_ref, x)]
        loads += load_side_by_side(move, m_refs, mixed_v)
        loads += load_rows(move, w_refs, w.at[0], pl.ds(0, width))
        load_next = load_rows(move, w_refs, w.at[1], pl.ds(width, width))
        load_last = load_rows(move, l_refs, w_last) + [move.start(col_ref, col)]
        wait_all(loads)
        rows = [p[i : i + 1, :].astype(F32) for i in range(9)]
        for part in tiles_of(count, tile):
            attended = x[part, :].astype(F32) + dot_nn(mixed_v[part, :], w[0]) + rows[5]
            rest[part, :] = attended
            z, _ = normal_rows(attended)
            n[part, :] = (z * rows[1] + rows[6]).astype(BF16)
        wait_all(load_next)
        for index, part in enumerate(tiles_of(count, tile)):
            hidden = dot_nn(n[part, :], w[1]) + rows[7]
            active = gelu_parts(hidden)[0].astype(BF16)
            if index == 0:
                wait_all(load_last)
            result = rest[part, :] + dot_nn(active, w_last[...]) + rows[8]
            y[part, :] = jnp.where(col[part, 0:1] < 3, result, 0.0).astype(BF16)
        place = 0
        for out in y_outs:
            move.put(y.at[pl.ds(place, out.shape[0])], out)
            place += out.shape[0]
        move.finish()

    buf = pltpu.VMEM((count, width), BF16)
    return kernel_call(
        body, "mlp_fwd", (latents, *mixed, *weight, *last, params, ids_col),
        [ANY] * (3 + split + 2 * pieces),
        [sds((rows, width)) for rows in cuts],
        [buf, buf, pltpu.VMEM((2, width, width), BF16), pltpu.VMEM((width, width), BF16),
         pltpu.VMEM(params.shape, BF16), pltpu.VMEM(ids_col.shape, jnp.int32),
         pltpu.VMEM((count, width), F32), buf, buf],
        3 + split + 24 + len(cuts), 6 * count * width * width,
    )


def middle_stash(latents, arrived, mixed, weight, last, params, ids_col, sides):
    count, width = latents.shape
    pieces = len(weight)
    split = len(mixed)
    tile = count // 4
    wide = width // 4

    def body(*refs):
        g_refs, refs = refs[: len(arrived)], refs[len(arrived) - 1 :]
        x_ref = refs[1]
        m_refs = refs[2 : 2 + split]
        w_refs = refs[2 + split : 2 + split + pieces]
        l_refs = refs[2 + split + pieces : 2 + split + 2 * pieces]
        p_ref, col_ref, d_out, m_out, t_out = refs[2 + split + 2 * pieces : 7 + split + 2 * pieces]
        grads = refs[7 + split + 2 * pieces : 7 + split + 2 * pieces + sides]
        (x, cot, mixed_v, w, w_last, p, col, n, z_v, r_v, act, slope_v, dhid, datt, dattn, dmix,
         terms, out_terms, sums, extra, sems) = refs[7 + split + 2 * pieces + sides :]
        move = Mover(sems)
        loads = [move.start(p_ref, p), move.start(x_ref, x)]
        loads += load_side_by_side(move, m_refs, mixed_v)
        loads += load_rows(move, w_refs, w.at[0], pl.ds(0, width))
        load_next = load_rows(move, w_refs, w.at[1], pl.ds(width, width))
        load_back, place = [move.start(col_ref, col)], 0
        for ref in g_refs:
            load_back.append(move.start(ref, cot.at[pl.ds(place, ref.shape[0])]))
            place += ref.shape[0]
        load_last = load_rows(move, l_refs, w_last)
        wait_all(loads)
        rows = [p[i : i + 1, :].astype(F32) for i in range(9)]
        for index, part in enumerate(tiles_of(count, tile)):
            attended = x[part, :].astype(F32) + dot_nn(mixed_v[part, :], w[0]) + rows[5]
            z, root = normal_rows(attended)
            z_v[part, :] = z.astype(BF16)
            r_v[part, :] = jnp.broadcast_to(root, (tile, 128))
            n[part, :] = (z * rows[1] + rows[6]).astype(BF16)
            if index == 0:
                wait_all(load_next)
            hidden = dot_nn(n[part, :], w[1]) + rows[7]
            active, slope = gelu_parts(hidden)
            act[part, :] = active.astype(BF16)
            slope_v[part, :] = slope.astype(BF16)
        wait_all(load_back)
        cot[...] = jnp.where(col[:, 0:1] < 3, cot[...].astype(F32), 0.0).astype(BF16)
        wait_all(load_last)
        totals = [jnp.zeros((1, width), F32) for _ in range(5)]
        for index, part in enumerate(tiles_of(count, tile)):
            dactive = dot_nt(cot[part, :], w_last[...])
            held = (slope_v[part, :].astype(F32) * dactive).astype(BF16)
            dhid[part, :] = held
            totals[3] += column_sum(held.astype(F32))
            totals[4] += column_sum(cot[part, :].astype(F32))
            block = pl.ds(index * wide, wide)
            terms[block, width:] = dot_tn(act[:, block], cot[...]).astype(BF16)
        move.put(terms.at[:, pl.ds(width, width)], t_out.at[:, pl.ds(width, width)])
        for index, part in enumerate(tiles_of(count, tile)):
            dnormed = dot_nt(dhid[part, :], w[1])
            z = z_v[part, :].astype(F32)
            totals[0] += column_sum(dnormed * z)
            totals[1] += column_sum(dnormed)
            dz = dnormed * rows[1]
            inner = dz - jnp.mean(dz, axis=-1, keepdims=True)
            inner = inner - z * jnp.mean(dz * z, axis=-1, keepdims=True)
            dattended = cot[part, :].astype(F32) + r_v[part, 0:1] * inner
            datt[part, :] = dattended
            held = dattended.astype(BF16)
            dattn[part, :] = held
            totals[2] += column_sum(held.astype(F32))
            block = pl.ds(index * wide, wide)
            terms[block, :width] = dot_tn(n[:, block], dhid[...]).astype(BF16)
            dmix[part, :] = dot_nt(held, w[0]).astype(BF16)
            move.put(datt.at[part], d_out.at[part])
            move.put(dmix.at[part], m_out.at[part])
        move.put(terms.at[:, pl.ds(0, width)], t_out.at[:, pl.ds(0, width)])
        for index in range(5):
            sums[index : index + 1, :] = totals[index]
        sums[5:PARAM_ROWS, :] = jnp.zeros((PARAM_ROWS - 5, width), F32)
        extra[...] = sums[...].astype(BF16)
        out_terms[...] = dot_tn(mixed_v[...], dattn[...]).astype(BF16)
        store_rows(move, out_terms, grads, extra)
        move.finish()

    buf = pltpu.VMEM((count, width), BF16)
    square = pltpu.VMEM((width, width), BF16)
    return kernel_call(
        body, "middle_stash", (*arrived, latents, *mixed, *weight, *last, params, ids_col),
        [ANY] * (3 + len(arrived) + split + 2 * pieces),
        [sds((count, width), F32), sds((count, width)), sds((width, 2 * width))]
        + term_shapes(width, width, sides),
        [buf, buf, buf, pltpu.VMEM((2, width, width), BF16), square, pltpu.VMEM(params.shape, BF16),
         pltpu.VMEM(ids_col.shape, jnp.int32), buf, buf, pltpu.VMEM((count, 128), F32), buf, buf, buf,
         pltpu.VMEM((count, width), F32), buf, buf, pltpu.VMEM((width, 2 * width), BF16), square,
         pltpu.VMEM((PARAM_ROWS, width), F32), pltpu.VMEM((PARAM_ROWS, width), BF16)],
        3 + len(arrived) + split + 24 + 8 + 2 + 2 * lax.axis_size("dp"), 16 * count * width * width,
    )


def attention_backward(saved, dmixed, z_rows, first_head, heads, sides):
    count, width = z_rows.shape
    side = heads * HEAD
    tile = count // 2
    cuts, at = [], 0
    for index, arrays in enumerate(saved):
        own = arrays[0].shape[1] // HEAD
        low, high = max(first_head, at), min(first_head + heads, at + own)
        if low < high:
            cuts.append((index, low - at, low - first_head, high - low))
        at += own
    saved = [saved[cut[0]] for cut in cuts]
    groups = len(saved)

    def body(*refs):
        inputs = [refs[6 * i : 6 * i + 6] for i in range(groups)]
        m_ref, n_ref, d_out = refs[6 * groups : 6 * groups + 3]
        grads = refs[6 * groups + 3 : 6 * groups + 3 + sides]
        q, k, v, o, e, inv, dmix, n, dqkv, dscore, terms, sums, extra, sems = refs[
            6 * groups + 3 + sides :
        ]
        move = Mover(sems)
        load_m = move.start(m_ref.at[:, pl.ds(first_head * HEAD, side)], dmix)
        small, large = [], []
        for (q_ref, k_ref, v_ref, o_ref, e_ref, l_ref), cut in zip(inputs, cuts, strict=True):
            _, low, place, own = cut
            source = pl.ds(low * HEAD, own * HEAD)
            lanes = pl.ds(place * HEAD, own * HEAD)
            loads = [
                move.start(ref.at[:, source], target.at[:, lanes])
                for ref, target in ((l_ref, inv), (o_ref, o), (v_ref, v))
            ]
            for head in range(own):
                large.append(move.start(e_ref.at[low + head], e.at[place + head]))
            loads += [
                move.start(ref.at[:, source], target.at[:, lanes])
                for ref, target in ((k_ref, k), (q_ref, q))
            ]
            small += [loads] + [[]] * (own - 1)
        load_n = move.start(n_ref, n)
        load_m.wait()
        for head in range(heads):
            lanes = pl.ds(head * HEAD, HEAD)
            wait_all(small[head])
            scaled = (dmix[:, lanes].astype(F32) * inv[:, lanes]).astype(BF16)
            row_sum = jnp.sum(scaled.astype(F32) * o[:, lanes].astype(F32), axis=1, keepdims=True)
            value_rows = v[:, lanes]
            head_keys = k[:, lanes]
            large[head].wait()
            for start in range(0, count, tile):
                part = pl.ds(start, tile)
                dprobs = dot_nt(scaled[start : start + tile], value_rows)
                held = e[head, part, :].astype(F32) * (dprobs - row_sum[start : start + tile])
                held = held.astype(BF16)
                dscore[part, :] = held
                dqkv[part, lanes] = (dot_nn(held, head_keys) * SCALE).astype(BF16)
            dqkv[:, pl.ds(side + head * HEAD, HEAD)] = (
                dot_tn(dscore[...], q[:, lanes]) * SCALE
            ).astype(BF16)
            dqkv[:, pl.ds(2 * side + head * HEAD, HEAD)] = dot_tn(e[head], scaled).astype(BF16)
        move.put(dqkv, d_out)
        sums[0:1, :] = column_sum(dqkv[...].astype(F32))
        sums[1:PARAM_ROWS, :] = jnp.zeros((PARAM_ROWS - 1, 3 * side), F32)
        extra[...] = sums[...].astype(BF16)
        load_n.wait()
        terms[...] = dot_tn(n[...], dqkv[...]).astype(BF16)
        store_rows(move, terms, grads, extra)
        move.finish()

    buf = pltpu.VMEM((count, side), BF16)
    return kernel_call(
        body, f"attention_backward_{first_head}",
        (*[array for group in saved for array in group], dmixed, z_rows),
        [ANY] * (6 * groups + 2),
        [sds((count, 3 * side))] + term_shapes(width, 3 * side, sides),
        [buf, buf, buf, buf, pltpu.VMEM((heads, count, count), BF16), pltpu.VMEM((count, side), F32),
         buf, pltpu.VMEM((count, width), BF16), pltpu.VMEM((count, 3 * side), BF16),
         pltpu.VMEM((count, count), BF16), pltpu.VMEM((width, 3 * side), BF16),
         pltpu.VMEM((PARAM_ROWS, 3 * side), F32), pltpu.VMEM((PARAM_ROWS, 3 * side), BF16)],
        2 + 5 * groups + heads + 1 + 2 * lax.axis_size("dp"), 2 * count * width * 3 * side + 16 * heads * count * count * HEAD,
    )


def input_backward(latents, dattended, parts, weights, params, results):
    count, width = latents.shape
    pieces = len(weights[0])
    groups = len(parts)
    total = len(weights)
    tile = count // 4

    def body(*refs):
        x_ref, d_ref = refs[:2]
        g_refs = refs[2 : 2 + groups]
        at = 2 + groups
        w_refs = [refs[at + i * pieces : at + (i + 1) * pieces] for i in range(total)]
        at += total * pieces
        r_refs = refs[at : at + len(results)]
        at += len(results)
        p_ref, y_out, r_out, x, datt, dqkv, w, acc, y, r_v, p, sems = refs[at:]
        move = Mover(sems)
        loads = []
        for kind in range(3):
            own_loads = []
            place = 0
            for ref in g_refs:
                own = ref.shape[1] // 3
                own_loads.append(
                    move.start(ref.at[:, pl.ds(kind * own, own)], dqkv.at[kind, :, pl.ds(place, own)])
                )
                place += own
            place = 0
            for ref in w_refs:
                own = ref[0].shape[1] // 3
                own_loads += load_rows(
                    move, ref, w.at[kind, :, pl.ds(place, own)], pl.ds(kind * own, own), width // 8
                )
                place += own
            loads.append(own_loads)
        late = [move.start(x_ref, x), move.start(d_ref, datt), move.start(p_ref, p)]
        back, place = [], 0
        for ref in r_refs:
            back.append(move.start(ref, r_v.at[pl.ds(place, ref.shape[0])]))
            place += ref.shape[0]
        for kind in range(2):
            wait_all(loads[kind])
            for part in tiles_of(count, tile):
                dnormed = dot_nt(dqkv[kind, part, :], w[kind])
                acc[part, :] = dnormed if kind == 0 else acc[part, :] + dnormed
        wait_all(loads[2] + late)
        gain = p[0:1, :].astype(F32)
        for part in tiles_of(count, tile):
            dnormed = acc[part, :] + dot_nt(dqkv[2, part, :], w[2])
            z, root = normal_rows(x[part, :].astype(F32))
            dz = dnormed * gain
            inner = dz - jnp.mean(dz, axis=-1, keepdims=True)
            inner = inner - z * jnp.mean(dz * z, axis=-1, keepdims=True)
            y[part, :] = (datt[part, :] + root * inner).astype(BF16)
            move.put(y.at[part], y_out.at[part])
        wait_all(back)
        move.put(r_v, r_out)
        move.finish()

    buf = pltpu.VMEM((count, width), BF16)
    return kernel_call(
        body, "input_backward",
        (latents, dattended, *parts, *[piece for weight in weights for piece in weight], *results,
         params),
        [ANY] * (3 + groups + total * pieces + len(results)),
        [sds((count, width)), sds((count, width))],
        [buf, pltpu.VMEM((count, width), F32), pltpu.VMEM((3, count, width), BF16),
         pltpu.VMEM((3, width, width), BF16), pltpu.VMEM((count, width), F32), buf, buf,
         pltpu.VMEM(params.shape, BF16)],
        3 + 3 * groups + 24 * total + len(results) + 5, 6 * count * width * width,
    )


def swapped(value, axis, flip):
    count = lax.axis_size(axis)
    return lax.ppermute(value, axis, [(source, source ^ flip) for source in range(count)])


def shifted(value, axis, steps):
    count = lax.axis_size(axis)
    pairs = [(source, (source + steps) % count) for source in range(count)]
    return lax.ppermute(value, axis, pairs)


def after(value, *others):
    return lax.optimization_barrier((value, *others))[0]


def all_after(values, *markers):
    return lax.optimization_barrier((*values, *markers))[: len(values)]


def send_rows(shard):
    if lax.axis_size("dp") != 8:
        return (lax.all_gather(shard, "dp", axis=0, tiled=True),)
    return tuple(swapped(shard, "dp", flip) for flip in (2, 4, 6))


def join_rows(shard, arrived):
    if len(arrived) == 1:
        return arrived
    side = jnp.concatenate([shard, *arrived], axis=0)
    return side, swapped(side, "dp", 1)


def added(*values):
    total = values[0].astype(F32)
    for value in values[1:]:
        total = total + value.astype(F32)
    return total


def sum_stages(pieces):
    if lax.axis_size("dp") != 8:
        shard = lax.psum_scatter(pieces[0], "dp", scatter_dimension=0, tiled=True)
        shard = lax.psum(shard, "pipe")
        (shard,) = yield (), (shard,)
        yield None, shard.astype(F32)
        return
    mine, theirs = pieces
    (other,) = yield (theirs,), (swapped(theirs, "dp", 1),)
    rows = mine.shape[0] // 4
    pair = []
    for step in range(4):
        part = slice(step * rows, (step + 1) * rows)
        pair.append(added(mine[part], other[part]).astype(BF16))
    arrived = yield pair, tuple(swapped(pair[step], "dp", 2 * step) for step in (1, 2, 3))
    shard = added(pair[0], *arrived).astype(BF16)
    flip = 1
    while flip < lax.axis_size("pipe"):
        (other,) = yield (shard,), (swapped(shard, "pipe", flip),)
        flip *= 2
        shard = added(shard, other)
        if flip < lax.axis_size("pipe"):
            shard = shard.astype(BF16)
    yield None, shard


def line_stages(shard):
    count = lax.axis_size("pipe")
    if count != 4:
        yield None, lax.psum(shard, "pipe").astype(F32)
        return
    (other,) = yield (shard,), (lax.ppermute(shard, "pipe", [(0, 1), (3, 2)]),)
    shard = added(shard, other).astype(BF16)
    (other,) = yield (shard,), (lax.ppermute(shard, "pipe", [(1, 2), (2, 1)]),)
    shard = added(shard, other).astype(BF16)
    (other,) = yield (shard,), (lax.ppermute(shard, "pipe", [(1, 0), (2, 3)]),)
    place = lax.axis_index("pipe")
    yield None, jnp.where((place == 0) | (place == 3), other, shard).astype(F32)


class Chunk:
    def __init__(self, terms, stages=sum_stages):
        self.stages = stages(terms)
        self.sent, self.result = next(self.stages)

    def step(self, marker=None):
        if self.sent is None:
            return ()
        arrived = self.result if marker is None else all_after(self.result, marker)
        self.sent, self.result = self.stages.send(arrived)
        return (self.result,) if self.sent is None else self.sent

    def finish(self):
        while self.sent is not None:
            self.step()
        return self.result


def local(
    fwd_latents,
    fwd_segments,
    stash_latents,
    stash_segments,
    upstream_grad,
    qkv_weight,
    out_weight,
    mlp_weight,
    norm_gain,
    biases,
):
    fwd_x, stash_x = fwd_latents[0], stash_latents[0]
    count, width = fwd_x.shape
    pieces = 2 if lax.axis_size("dp") == 8 else 1
    fwd_row, stash_row = fwd_segments, stash_segments
    fwd_col = jnp.broadcast_to(fwd_segments[0][:, None], (count, 128))
    stash_col = jnp.broadcast_to(stash_segments[0][:, None], (count, 128))
    own = norm_gain.shape[1]
    small = jnp.concatenate(
        [norm_gain, biases, jnp.zeros((PARAM_ROWS - 9, own), norm_gain.dtype)], axis=0
    )

    def qkv_shard(first, heads):
        cut = qkv_weight[:, :, first * HEAD : (first + heads) * HEAD]
        return jnp.concatenate([cut[0], cut[1], cut[2]], axis=1)

    first_shard = qkv_shard(*FORWARD_GROUPS[0])
    if pieces == 2:
        small = jnp.pad(small, ((0, 0), (0, first_shard.shape[1] - own)))
        first_shard = jnp.concatenate([first_shard, small], axis=0)
    qkv_shards = [first_shard] + [qkv_shard(*group) for group in FORWARD_GROUPS[1:]]
    flights = []
    for shard in qkv_shards:
        if flights:
            shard = after(shard, *flights[-1])
        flights.append(send_rows(shard))
    middle = jnp.concatenate([out_weight, mlp_weight[0]], axis=1)
    middle = (lax.all_gather(after(middle, *flights[0]), "dp", axis=0, tiled=True),)
    last = (lax.all_gather(mlp_weight[1], "dp", axis=0, tiled=True),)
    flights[0] = all_after(flights[0], stash_col, fwd_col)
    gathered = [join_rows(qkv_shards[0], flights[0])]
    if pieces == 1:
        params = lax.all_gather(small, "dp", axis=1, tiled=True)
    else:
        params = None
    half = count // 32 * 16
    upstream = upstream_grad[0]
    cotangent = [shifted(upstream[:half], "pipe", -1), shifted(upstream[half:], "pipe", -1)]

    saved, fwd_mixed = [], []
    normed = (stash_x, fwd_x)
    if params is not None:
        plain = [normal_rows(rows.astype(F32))[0] for rows in normed]
        z_rows = plain[0].astype(BF16)
        normed = tuple(
            (rows * params[0:1].astype(F32) + params[2:3].astype(F32)).astype(BF16)
            for rows in plain
        )
    for index, (first, heads) in enumerate(FORWARD_GROUPS):
        (kept, plain), extra = attention_group(
            [(normed[0], stash_col, stash_row, True), (normed[1], fwd_col, fwd_row, False)],
            gathered[index], params, first, heads,
        )
        if extra:
            normed, z_rows, params = tuple(extra[:2]), extra[2], extra[3]
        saved.append(kept)
        fwd_mixed.append(plain[0])
        here = ()
        if index:
            here = all_after((cotangent[index - 1],), plain[0])
            cotangent[index - 1] = here[0]
        if index + 1 < len(FORWARD_GROUPS):
            arrived = all_after(flights[index + 1], plain[0], *here)
            gathered.append(join_rows(qkv_shards[index + 1], arrived))
    stash_mixed = [group[3] for group in saved]
    dattended, dmixed, mlp_terms, *terms = middle_stash(
        stash_x, cotangent, stash_mixed, middle, last, params, stash_col, pieces
    )
    mlp_part = lax.psum_scatter(mlp_terms, "dp", scatter_dimension=0, tiled=True)
    running = [Chunk(terms)]

    def advance(marker):
        return [value for chunk in running for value in chunk.step(marker)]

    def begin(terms, sent):
        running.append(Chunk([*terms[:-1], after(terms[-1], *sent)]))
        return running[-1].step()

    result = mlp_fwd(
        after(fwd_x, dmixed), fwd_mixed, middle, last, params, fwd_col, (half, count - half)
    )
    latents = [shifted(rows, "pipe", 1) for rows in result]
    sent = advance(result[0])
    dprojected = []
    for index, (first, heads) in enumerate(BACKWARD_GROUPS):
        part, *terms = attention_backward(
            saved, after(dmixed, *sent), z_rows, first, heads, pieces
        )
        dprojected.append(part)
        sent = advance(part)
        if index < 2:
            (latents[index],) = all_after((latents[index],), part)
            sent.append(latents[index])
        if index == 1:
            (mlp_part,) = all_after((mlp_part,), part)
            mlp_total = lax.psum(mlp_part, "pipe")
            sent.append(mlp_part)
        sent += begin(terms, sent)
        dmixed = after(dmixed, part)
    input_grad, latents = input_backward(
        after(stash_x, *sent), dattended, dprojected, gathered, params, latents
    )
    sent = advance(input_grad)
    (mlp_total,) = all_after((mlp_total,), input_grad, *running[-1].step())
    mlp_total = mlp_total.astype(F32)
    out_total, *qkv_totals = [chunk.finish() for chunk in running]

    rows = qkv_weight.shape[1]
    gain = norm_gain[0].astype(F32)[:, None]
    shift = biases[0].astype(F32)[:, None]
    grads, sums, gain_first, shift_first = [], [], 0.0, 0.0
    for kind in range(3):
        cut = [
            total[:, kind * total.shape[1] // 3 : (kind + 1) * total.shape[1] // 3]
            for total in qkv_totals
        ]
        cut = jnp.concatenate(cut, axis=1)
        weight = qkv_weight[kind].astype(F32)
        grads.append(gain * cut[:rows] + shift * cut[rows : rows + 1])
        sums.append(cut[rows : rows + 1])
        gain_first += jnp.sum(weight * cut[:rows], axis=1)
        shift_first += jnp.sum(weight * cut[rows : rows + 1], axis=1)
    place = lax.axis_index("dp") * rows

    def own_part(row):
        return lax.dynamic_slice_in_dim(row, place, rows, axis=row.ndim - 1)

    late = own_part(out_total[rows : rows + 5])
    gain_grad = jnp.stack([gain_first, late[0]])
    bias_grad = jnp.stack(
        [shift_first, own_part(sums[0][0]), own_part(sums[2][0]), late[2], late[1], late[3], late[4]]
    )
    return (
        latents[None],
        input_grad[None],
        jnp.stack(grads),
        out_total[:rows],
        jnp.stack([mlp_total[:, :width], mlp_total[:, width:]]),
        gain_grad,
        bias_grad,
        late[1],
    )


def solution(mesh):
    in_specs = (
        P("pipe", "dp", None),
        P("pipe", "dp"),
        P("pipe", "dp", None),
        P("pipe", "dp"),
        P("pipe", "dp", None),
        P(None, "dp", None),
        P("dp", None),
        P(None, "dp", None),
        P(None, "dp"),
        P(None, "dp"),
    )
    out_specs = (
        P("pipe", "dp", None),
        P("pipe", "dp", None),
        P(None, "dp", None),
        P("dp", None),
        P(None, "dp", None),
        P(None, "dp"),
        P(None, "dp"),
        P("dp"),
    )
    return jax.shard_map(local, mesh=mesh, in_specs=in_specs, out_specs=out_specs, check_vma=False)
```

```python
import functools

import jax
import jax.numpy as jnp
from jax import lax
from jax.experimental import pallas as pl
from jax.experimental.pallas import tpu as pltpu
from jax.sharding import PartitionSpec as P

HEADS = 8
HEAD = 128
EPSILON = 1e-05
SCALE = HEAD ** (-0.5)
LOG2E = 1.4426950408889634
GELU_C = 0.7978845608028654
GELU_A = 0.044715
FORWARD_GROUPS = ((0, 1), (1, 3), (4, 4))
BACKWARD_GROUPS = ((0, 3), (3, 3), (6, 2))
VMEM_LIMIT = 56 * 2**20
PARAM_ROWS = 16

F32 = jnp.float32
BF16 = jnp.bfloat16
ANY = pl.BlockSpec(memory_space=pl.ANY)
VMEM = pl.BlockSpec(memory_space=pltpu.VMEM)


def sds(shape, dtype=BF16):
    return jax.ShapeDtypeStruct(shape, dtype)


def dot_nn(a, b):
    return jnp.dot(a, b, preferred_element_type=F32)


def dot_nt(a, b):
    return lax.dot_general(a, b, (((1,), (1,)), ((), ())), preferred_element_type=F32)


def dot_tn(a, b):
    return lax.dot_general(a, b, (((0,), (0,)), ((), ())), preferred_element_type=F32)


class Mover:
    def __init__(self, sems):
        self.sems = sems
        self.used = 0
        self.open = []

    def start(self, source, target):
        copy = pltpu.make_async_copy(source, target, self.sems.at[self.used])
        self.used += 1
        copy.start()
        return copy

    def put(self, source, target):
        self.open.append(self.start(source, target))

    def finish(self):
        for copy in self.open:
            copy.wait()


def load_rows(move, pieces, target, columns=None, rows=None):
    columns = pl.ds(0, target.shape[1]) if columns is None else columns
    if len(pieces) == 1:
        return [move.start(pieces[0].at[pl.ds(0, target.shape[0]), columns], target)]
    mine = lax.axis_index("dp")
    step_rows = pieces[0].shape[0] // 4
    rows = step_rows if rows is None else rows
    copies = []
    for step in range(4):
        for side in range(2):
            owner = mine ^ (2 * step + side)
            source = pieces[side].at[pl.ds(step * step_rows, rows), columns]
            copies.append(
                move.start(source, target.at[pl.ds(pl.multiple_of(owner * rows, rows), rows)])
            )
    return copies


def load_side_by_side(move, refs, target):
    copies, place = [], 0
    for ref in refs:
        copies.append(move.start(ref, target.at[:, pl.ds(place, ref.shape[1])]))
        place += ref.shape[1]
    return copies


def store_rows(move, source, pieces, extra):
    count = lax.axis_size("dp")
    rows = source.shape[0] // count
    whole = rows + extra.shape[0]
    mine = lax.axis_index("dp")
    for index in range(count):
        if len(pieces) == 1:
            owner, target, place = index, pieces[0], index
        else:
            owner, target, place = mine ^ index, pieces[index % 2], index // 2
        start = pl.multiple_of(owner * rows, rows)
        move.put(source.at[pl.ds(start, rows)], target.at[pl.ds(place * whole, rows)])
        move.put(extra, target.at[pl.ds(place * whole + rows, extra.shape[0])])


def term_shapes(width, columns, sides):
    count = lax.axis_size("dp")
    return [sds(((width + count * PARAM_ROWS) // sides, columns))] * sides


def wait_all(copies):
    for copy in copies:
        copy.wait()


def tiles_of(count, size):
    return [pl.ds(start, min(size, count - start)) for start in range(0, count, size)]


def normal_rows(rows):
    centred = rows - jnp.mean(rows, axis=-1, keepdims=True)
    root = lax.rsqrt(jnp.mean(centred * centred, axis=-1, keepdims=True) + EPSILON)
    return centred * root, root


def column_sum(rows):
    return jnp.sum(rows, axis=0, keepdims=True)


def kernel_call(body, name, inputs, in_specs, outs, scratch, copies, flops):
    moved = sum(a.size * a.dtype.itemsize for a in inputs)
    moved += sum(int(jnp.dtype(o.dtype).itemsize) * functools.reduce(int.__mul__, o.shape) for o in outs)
    return pl.pallas_call(
        body,
        name=name,
        out_shape=outs,
        in_specs=in_specs,
        out_specs=[ANY] * len(outs),
        scratch_shapes=list(scratch) + [pltpu.SemaphoreType.DMA((copies,))],
        compiler_params=pltpu.CompilerParams(vmem_limit_bytes=VMEM_LIMIT),
        cost_estimate=pl.CostEstimate(flops=int(flops), bytes_accessed=int(moved), transcendentals=0),
    )(*inputs)


def load_params(move, pieces, rows, target):
    mine = lax.axis_index("dp")
    step_rows = pieces[0].shape[0] // 4
    width = target.shape[1] // 8
    copies = []
    for step in range(4):
        for side in range(2):
            owner = mine ^ (2 * step + side)
            copies.append(
                move.start(
                    pieces[side].at[pl.ds(step * step_rows + rows, PARAM_ROWS), pl.ds(0, width)],
                    target.at[:, pl.ds(pl.multiple_of(owner * width, width), width)],
                )
            )
    return copies


def attention_group(batches, weight, params, first_head, heads):
    count, width = batches[0][0].shape
    side = heads * HEAD
    pieces = len(weight)
    total = len(batches)
    tile = count // 2
    opening = params is None
    own_rows = width // 8 if pieces == 2 else width

    def body(*refs):
        each = 2 if opening else 3
        inputs = [refs[each * i : each * (i + 1)] for i in range(total)]
        w_refs = refs[each * total : each * total + pieces]
        at = each * total + pieces
        if not opening:
            p_ref = refs[at]
            at += 1
        outputs = []
        for _, _, _, keep in batches:
            outputs.append(refs[at : at + (6 if keep else 1)])
            at += 6 if keep else 1
        if opening:
            normed_outs = refs[at : at + total]
            col_outs = refs[at + total : at + 2 * total]
            z_out, p_out = refs[at + 2 * total : at + 2 * total + 2]
            at += 2 * total + 2
        params_v, w_v, *held = refs[at:-1]
        if opening:
            z_v, *held = held
        move = Mover(refs[-1])
        if not opening:
            loads = [move.start(p_ref, params_v)]
        else:
            loads = load_params(move, w_refs, own_rows, params_v)
        scratch, batch_loads = [], []
        for index, (_, _, _, keep) in enumerate(batches):
            scratch.append(held[: 9 if keep else 7])
            held = held[9 if keep else 7 :]
            normed_v, col_v, row_v = scratch[index][:3]
            batch_loads.append(move.start(inputs[index][0], normed_v))
            if index == 0:
                w_loads = load_rows(move, w_refs, w_v, rows=own_rows)
            ids = [move.start(inputs[index][1], row_v)]
            if not opening:
                ids.append(move.start(inputs[index][2], col_v))
            scratch[index] = (*scratch[index], ids)
        wait_all(loads)
        if opening:
            move.put(params_v, p_out)
        at = first_head * HEAD
        q_shift = params_v[3:4, at : at + side].astype(F32)
        v_shift = params_v[4:5, at : at + side].astype(F32)
        for index, (_, _, _, keep) in enumerate(batches):
            normed_v, col_v, row_v, q, k, v, o = scratch[index][:7]
            batch_loads[index].wait()
            if opening:
                gain = params_v[0:1, :].astype(F32)
                shift = params_v[2:3, :].astype(F32)
                for part in tiles_of(count, 208):
                    z, _ = normal_rows(normed_v[part, :].astype(F32))
                    normed_v[part, :] = (z * gain + shift).astype(BF16)
                    if keep:
                        z_v[part, :] = z.astype(BF16)
                move.put(normed_v, normed_outs[index])
                if keep:
                    move.put(z_v, z_out)
                wait_all(scratch[index][-1])
                top = lax.broadcasted_iota(jnp.int32, (16, count), 0) == 0
                spread = jnp.where(top, row_v[...].astype(F32), 0.0).astype(BF16)
                col_v[...] = dot_tn(spread, jnp.ones((16, 128), BF16))
                move.put(col_v, col_outs[index])
            if index == 0:
                wait_all(w_loads)
            for part in tiles_of(count, tile):
                projected = dot_nn(normed_v[part, :], w_v[...])
                q[part, :] = (projected[:, :side] + q_shift).astype(BF16)
                k[part, :] = projected[:, side : 2 * side].astype(BF16)
                v[part, :] = (projected[:, 2 * side :] + v_shift).astype(BF16)
            if keep:
                q_out, k_out, v_out, o_out, e_out, l_out = outputs[index]
                e_all, inv = scratch[index][7:9]
                move.put(q, q_out)
                move.put(k, k_out)
                move.put(v, v_out)
            else:
                o_out = outputs[index][0]
            if not opening:
                wait_all(scratch[index][-1])
            row = row_v[...].astype(F32)
            for head in range(heads):
                lanes = pl.ds(head * HEAD, HEAD)
                key_rows = k[:, lanes]
                value_rows = v[:, lanes]
                wide = jnp.concatenate([value_rows, jnp.ones_like(value_rows)], axis=1)
                for part in tiles_of(count, tile):
                    scores = dot_nt(q[part, lanes], key_rows)
                    scores = jnp.where(col_v[part, 0:1] == row, scores, -1e30)
                    top = jnp.max(scores, axis=1, keepdims=True)
                    e = jnp.exp2(scores * (SCALE * LOG2E) - top * (SCALE * LOG2E)).astype(BF16)
                    if keep:
                        e_all[head, part, :] = e
                    both = dot_nn(e, wide)
                    inverse = 1.0 / both[:, HEAD:]
                    if keep:
                        inv[part, lanes] = inverse
                    o[part, lanes] = (both[:, :HEAD] * inverse).astype(BF16)
                if keep:
                    move.put(e_all.at[head], e_out.at[head])
            move.put(o, o_out)
            if keep:
                move.put(inv, l_out)
        move.finish()

    buf = pltpu.VMEM((count, side), BF16)
    scratch = [pltpu.VMEM((PARAM_ROWS, width), BF16), pltpu.VMEM((width, 3 * side), BF16)]
    scratch += [pltpu.VMEM((count, width), BF16)] if opening else []
    outs, inputs = [], []
    for normed, ids_col, ids_row, keep in batches:
        inputs += [normed, ids_row] if opening else [normed, ids_row, ids_col]
        scratch += [
            pltpu.VMEM((count, width), BF16), pltpu.VMEM((count, 128), F32),
            pltpu.VMEM(ids_row.shape, jnp.int32), buf, buf, buf, buf,
        ]
        outs += [sds((count, side))]
        if keep:
            scratch += [pltpu.VMEM((heads, count, count), BF16), pltpu.VMEM((count, side), F32)]
            outs += [sds((count, side))] * 3 + [sds((heads, count, count)), sds((count, side), F32)]
    if opening:
        outs += [sds((count, width))] * total + [sds((count, 128), F32)] * total
        outs += [sds((count, width)), sds((PARAM_ROWS, width))]
    flops = total * (2 * count * width * 3 * side + 8 * heads * count * count * HEAD)
    result = kernel_call(
        body, f"attention_{'_'.join('stash' if b[3] else 'fwd' for b in batches)}_{first_head}",
        (*inputs, *weight, *([] if opening else [params])),
        [ANY] * ((2 if opening else 3) * total + pieces + (0 if opening else 1)), outs, scratch,
        19 + total * (5 + 5 + heads), flops,
    )
    split = []
    for _, _, _, keep in batches:
        split.append(result[: 6 if keep else 1])
        result = result[6 if keep else 1 :]
    return split, result


def gelu_parts(hidden):
    square = hidden * hidden
    bend = jnp.tanh(GELU_C * hidden * (1.0 + GELU_A * square))
    half = 0.5 * (1.0 + bend)
    slope = half + 0.5 * hidden * (1.0 - bend * bend) * (GELU_C * (1.0 + 3.0 * GELU_A * square))
    return hidden * half, slope


def mlp_fwd(latents, mixed, weight, last, params, ids_col, cuts):
    count, width = latents.shape
    pieces = len(weight)
    split = len(mixed)
    tile = count // 4

    def body(*refs):
        x_ref = refs[0]
        m_refs = refs[1 : 1 + split]
        w_refs = refs[1 + split : 1 + split + pieces]
        l_refs = refs[1 + split + pieces : 1 + split + 2 * pieces]
        p_ref, col_ref = refs[1 + split + 2 * pieces : 3 + split + 2 * pieces]
        y_outs = refs[3 + split + 2 * pieces : 3 + split + 2 * pieces + len(cuts)]
        x, mixed_v, w, w_last, p, col, rest, n, y, sems = refs[3 + split + 2 * pieces + len(cuts) :]
        move = Mover(sems)
        loads = [move.start(p_ref, p), move.start(x_ref, x)]
        loads += load_side_by_side(move, m_refs, mixed_v)
        loads += load_rows(move, w_refs, w.at[0], pl.ds(0, width))
        load_next = load_rows(move, w_refs, w.at[1], pl.ds(width, width))
        load_last = load_rows(move, l_refs, w_last) + [move.start(col_ref, col)]
        wait_all(loads)
        rows = [p[i : i + 1, :].astype(F32) for i in range(9)]
        for part in tiles_of(count, tile):
            attended = x[part, :].astype(F32) + dot_nn(mixed_v[part, :], w[0]) + rows[5]
            rest[part, :] = attended
            z, _ = normal_rows(attended)
            n[part, :] = (z * rows[1] + rows[6]).astype(BF16)
        wait_all(load_next)
        for index, part in enumerate(tiles_of(count, tile)):
            hidden = dot_nn(n[part, :], w[1]) + rows[7]
            active = gelu_parts(hidden)[0].astype(BF16)
            if index == 0:
                wait_all(load_last)
            result = rest[part, :] + dot_nn(active, w_last[...]) + rows[8]
            y[part, :] = jnp.where(col[part, 0:1] < 3, result, 0.0).astype(BF16)
        place = 0
        for out in y_outs:
            move.put(y.at[pl.ds(place, out.shape[0])], out)
            place += out.shape[0]
        move.finish()

    buf = pltpu.VMEM((count, width), BF16)
    return kernel_call(
        body, "mlp_fwd", (latents, *mixed, *weight, *last, params, ids_col),
        [ANY] * (3 + split + 2 * pieces),
        [sds((rows, width)) for rows in cuts],
        [buf, buf, pltpu.VMEM((2, width, width), BF16), pltpu.VMEM((width, width), BF16),
         pltpu.VMEM(params.shape, BF16), pltpu.VMEM(ids_col.shape, F32),
         pltpu.VMEM((count, width), F32), buf, buf],
        3 + split + 24 + len(cuts), 6 * count * width * width,
    )


def middle_stash(latents, arrived, mixed, weight, last, params, ids_col, sides):
    count, width = latents.shape
    pieces = len(weight)
    split = len(mixed)
    tile = count // 4
    wide = width // 4

    def body(*refs):
        g_refs, refs = refs[: len(arrived)], refs[len(arrived) - 1 :]
        x_ref = refs[1]
        m_refs = refs[2 : 2 + split]
        w_refs = refs[2 + split : 2 + split + pieces]
        l_refs = refs[2 + split + pieces : 2 + split + 2 * pieces]
        p_ref, col_ref, d_out, m_out, t_out = refs[2 + split + 2 * pieces : 7 + split + 2 * pieces]
        grads = refs[7 + split + 2 * pieces : 7 + split + 2 * pieces + sides]
        (x, cot, mixed_v, w, w_last, p, col, n, z_v, r_v, act, slope_v, dhid, datt, dattn, dmix,
         terms, out_terms, sums, extra, sems) = refs[7 + split + 2 * pieces + sides :]
        move = Mover(sems)
        loads = [move.start(p_ref, p), move.start(x_ref, x)]
        loads += load_side_by_side(move, m_refs, mixed_v)
        loads += load_rows(move, w_refs, w.at[0], pl.ds(0, width))
        load_next = load_rows(move, w_refs, w.at[1], pl.ds(width, width))
        load_back, place = [move.start(col_ref, col)], 0
        for ref in g_refs:
            load_back.append(move.start(ref, cot.at[pl.ds(place, ref.shape[0])]))
            place += ref.shape[0]
        load_last = load_rows(move, l_refs, w_last)
        wait_all(loads)
        rows = [p[i : i + 1, :].astype(F32) for i in range(9)]
        for index, part in enumerate(tiles_of(count, tile)):
            attended = x[part, :].astype(F32) + dot_nn(mixed_v[part, :], w[0]) + rows[5]
            z, root = normal_rows(attended)
            z_v[part, :] = z.astype(BF16)
            r_v[part, :] = jnp.broadcast_to(root, (tile, 128))
            n[part, :] = (z * rows[1] + rows[6]).astype(BF16)
            if index == 0:
                wait_all(load_next)
            hidden = dot_nn(n[part, :], w[1]) + rows[7]
            active, slope = gelu_parts(hidden)
            act[part, :] = active.astype(BF16)
            slope_v[part, :] = slope.astype(BF16)
        wait_all(load_back)
        cot[...] = jnp.where(col[:, 0:1] < 3, cot[...].astype(F32), 0.0).astype(BF16)
        wait_all(load_last)
        totals = [jnp.zeros((1, width), F32) for _ in range(5)]
        for index, part in enumerate(tiles_of(count, tile)):
            dactive = dot_nt(cot[part, :], w_last[...])
            held = (slope_v[part, :].astype(F32) * dactive).astype(BF16)
            dhid[part, :] = held
            totals[3] += column_sum(held.astype(F32))
            totals[4] += column_sum(cot[part, :].astype(F32))
            block = pl.ds(index * wide, wide)
            terms[block, width:] = dot_tn(act[:, block], cot[...]).astype(BF16)
        move.put(terms.at[:, pl.ds(width, width)], t_out.at[:, pl.ds(width, width)])
        for index, part in enumerate(tiles_of(count, tile)):
            dnormed = dot_nt(dhid[part, :], w[1])
            z = z_v[part, :].astype(F32)
            totals[0] += column_sum(dnormed * z)
            totals[1] += column_sum(dnormed)
            dz = dnormed * rows[1]
            inner = dz - jnp.mean(dz, axis=-1, keepdims=True)
            inner = inner - z * jnp.mean(dz * z, axis=-1, keepdims=True)
            dattended = cot[part, :].astype(F32) + r_v[part, 0:1] * inner
            datt[part, :] = dattended
            held = dattended.astype(BF16)
            dattn[part, :] = held
            totals[2] += column_sum(held.astype(F32))
            block = pl.ds(index * wide, wide)
            terms[block, :width] = dot_tn(n[:, block], dhid[...]).astype(BF16)
            dmix[part, :] = dot_nt(held, w[0]).astype(BF16)
            move.put(datt.at[part], d_out.at[part])
            move.put(dmix.at[part], m_out.at[part])
        move.put(terms.at[:, pl.ds(0, width)], t_out.at[:, pl.ds(0, width)])
        for index in range(5):
            sums[index : index + 1, :] = totals[index]
        sums[5:PARAM_ROWS, :] = jnp.zeros((PARAM_ROWS - 5, width), F32)
        extra[...] = sums[...].astype(BF16)
        out_terms[...] = dot_tn(mixed_v[...], dattn[...]).astype(BF16)
        store_rows(move, out_terms, grads, extra)
        move.finish()

    buf = pltpu.VMEM((count, width), BF16)
    square = pltpu.VMEM((width, width), BF16)
    return kernel_call(
        body, "middle_stash", (*arrived, latents, *mixed, *weight, *last, params, ids_col),
        [ANY] * (3 + len(arrived) + split + 2 * pieces),
        [sds((count, width), F32), sds((count, width)), sds((width, 2 * width))]
        + term_shapes(width, width, sides),
        [buf, buf, buf, pltpu.VMEM((2, width, width), BF16), square, pltpu.VMEM(params.shape, BF16),
         pltpu.VMEM(ids_col.shape, F32), buf, buf, pltpu.VMEM((count, 128), F32), buf, buf, buf,
         pltpu.VMEM((count, width), F32), buf, buf, pltpu.VMEM((width, 2 * width), BF16), square,
         pltpu.VMEM((PARAM_ROWS, width), F32), pltpu.VMEM((PARAM_ROWS, width), BF16)],
        3 + len(arrived) + split + 24 + 8 + 2 + 2 * lax.axis_size("dp"), 16 * count * width * width,
    )


def attention_backward(saved, dmixed, z_rows, first_head, heads, sides):
    count, width = z_rows.shape
    side = heads * HEAD
    tile = count // 2
    cuts, at = [], 0
    for index, arrays in enumerate(saved):
        own = arrays[0].shape[1] // HEAD
        low, high = max(first_head, at), min(first_head + heads, at + own)
        if low < high:
            cuts.append((index, low - at, low - first_head, high - low))
        at += own
    saved = [saved[cut[0]] for cut in cuts]
    groups = len(saved)

    def body(*refs):
        inputs = [refs[6 * i : 6 * i + 6] for i in range(groups)]
        m_ref, n_ref, d_out = refs[6 * groups : 6 * groups + 3]
        grads = refs[6 * groups + 3 : 6 * groups + 3 + sides]
        q, k, v, o, e, inv, dmix, n, dqkv, dscore, terms, sums, extra, sems = refs[
            6 * groups + 3 + sides :
        ]
        move = Mover(sems)
        load_m = move.start(m_ref.at[:, pl.ds(first_head * HEAD, side)], dmix)
        small, large = [], []
        for (q_ref, k_ref, v_ref, o_ref, e_ref, l_ref), cut in zip(inputs, cuts, strict=True):
            _, low, place, own = cut
            source = pl.ds(low * HEAD, own * HEAD)
            lanes = pl.ds(place * HEAD, own * HEAD)
            loads = [
                move.start(ref.at[:, source], target.at[:, lanes])
                for ref, target in ((l_ref, inv), (o_ref, o), (v_ref, v))
            ]
            for head in range(own):
                large.append(move.start(e_ref.at[low + head], e.at[place + head]))
            loads += [
                move.start(ref.at[:, source], target.at[:, lanes])
                for ref, target in ((k_ref, k), (q_ref, q))
            ]
            small += [loads] + [[]] * (own - 1)
        load_n = move.start(n_ref, n)
        load_m.wait()
        for head in range(heads):
            lanes = pl.ds(head * HEAD, HEAD)
            wait_all(small[head])
            scaled = (dmix[:, lanes].astype(F32) * inv[:, lanes]).astype(BF16)
            row_sum = jnp.sum(scaled.astype(F32) * o[:, lanes].astype(F32), axis=1, keepdims=True)
            value_rows = v[:, lanes]
            head_keys = k[:, lanes]
            large[head].wait()
            for start in range(0, count, tile):
                part = pl.ds(start, tile)
                dprobs = dot_nt(scaled[start : start + tile], value_rows)
                held = e[head, part, :].astype(F32) * (dprobs - row_sum[start : start + tile])
                held = held.astype(BF16)
                dscore[part, :] = held
                dqkv[part, lanes] = (dot_nn(held, head_keys) * SCALE).astype(BF16)
            dqkv[:, pl.ds(side + head * HEAD, HEAD)] = (
                dot_tn(dscore[...], q[:, lanes]) * SCALE
            ).astype(BF16)
            dqkv[:, pl.ds(2 * side + head * HEAD, HEAD)] = dot_tn(e[head], scaled).astype(BF16)
        move.put(dqkv, d_out)
        sums[0:1, :] = column_sum(dqkv[...].astype(F32))
        sums[1:PARAM_ROWS, :] = jnp.zeros((PARAM_ROWS - 1, 3 * side), F32)
        extra[...] = sums[...].astype(BF16)
        load_n.wait()
        terms[...] = dot_tn(n[...], dqkv[...]).astype(BF16)
        store_rows(move, terms, grads, extra)
        move.finish()

    buf = pltpu.VMEM((count, side), BF16)
    return kernel_call(
        body, f"attention_backward_{first_head}",
        (*[array for group in saved for array in group], dmixed, z_rows),
        [ANY] * (6 * groups + 2),
        [sds((count, 3 * side))] + term_shapes(width, 3 * side, sides),
        [buf, buf, buf, buf, pltpu.VMEM((heads, count, count), BF16), pltpu.VMEM((count, side), F32),
         buf, pltpu.VMEM((count, width), BF16), pltpu.VMEM((count, 3 * side), BF16),
         pltpu.VMEM((count, count), BF16), pltpu.VMEM((width, 3 * side), BF16),
         pltpu.VMEM((PARAM_ROWS, 3 * side), F32), pltpu.VMEM((PARAM_ROWS, 3 * side), BF16)],
        2 + 5 * groups + heads + 1 + 2 * lax.axis_size("dp"), 2 * count * width * 3 * side + 16 * heads * count * count * HEAD,
    )


def input_backward(latents, dattended, parts, weights, params, results):
    count, width = latents.shape
    pieces = len(weights[0])
    groups = len(parts)
    total = len(weights)
    tile = count // 4

    def body(*refs):
        x_ref, d_ref = refs[:2]
        g_refs = refs[2 : 2 + groups]
        at = 2 + groups
        w_refs = [refs[at + i * pieces : at + (i + 1) * pieces] for i in range(total)]
        at += total * pieces
        r_refs = refs[at : at + len(results)]
        at += len(results)
        p_ref, y_out, r_out, x, datt, dqkv, w, acc, y, r_v, p, sems = refs[at:]
        move = Mover(sems)
        loads = []
        for kind in range(3):
            own_loads = []
            place = 0
            for ref in g_refs:
                own = ref.shape[1] // 3
                own_loads.append(
                    move.start(ref.at[:, pl.ds(kind * own, own)], dqkv.at[kind, :, pl.ds(place, own)])
                )
                place += own
            place = 0
            for ref in w_refs:
                own = ref[0].shape[1] // 3
                own_loads += load_rows(
                    move, ref, w.at[kind, :, pl.ds(place, own)], pl.ds(kind * own, own), width // 8
                )
                place += own
            loads.append(own_loads)
        late = [move.start(x_ref, x), move.start(d_ref, datt), move.start(p_ref, p)]
        back, place = [], 0
        for ref in r_refs:
            back.append(move.start(ref, r_v.at[pl.ds(place, ref.shape[0])]))
            place += ref.shape[0]
        for kind in range(2):
            wait_all(loads[kind])
            for part in tiles_of(count, tile):
                dnormed = dot_nt(dqkv[kind, part, :], w[kind])
                acc[part, :] = dnormed if kind == 0 else acc[part, :] + dnormed
        wait_all(loads[2] + late)
        gain = p[0:1, :].astype(F32)
        for part in tiles_of(count, tile):
            dnormed = acc[part, :] + dot_nt(dqkv[2, part, :], w[2])
            z, root = normal_rows(x[part, :].astype(F32))
            dz = dnormed * gain
            inner = dz - jnp.mean(dz, axis=-1, keepdims=True)
            inner = inner - z * jnp.mean(dz * z, axis=-1, keepdims=True)
            y[part, :] = (datt[part, :] + root * inner).astype(BF16)
            move.put(y.at[part], y_out.at[part])
        wait_all(back)
        move.put(r_v, r_out)
        move.finish()

    buf = pltpu.VMEM((count, width), BF16)
    return kernel_call(
        body, "input_backward",
        (latents, dattended, *parts, *[piece for weight in weights for piece in weight], *results,
         params),
        [ANY] * (3 + groups + total * pieces + len(results)),
        [sds((count, width)), sds((count, width))],
        [buf, pltpu.VMEM((count, width), F32), pltpu.VMEM((3, count, width), BF16),
         pltpu.VMEM((3, width, width), BF16), pltpu.VMEM((count, width), F32), buf, buf,
         pltpu.VMEM(params.shape, BF16)],
        3 + 3 * groups + 24 * total + len(results) + 5, 6 * count * width * width,
    )


def swapped(value, axis, flip):
    count = lax.axis_size(axis)
    return lax.ppermute(value, axis, [(source, source ^ flip) for source in range(count)])


def shifted(value, axis, steps):
    count = lax.axis_size(axis)
    pairs = [(source, (source + steps) % count) for source in range(count)]
    return lax.ppermute(value, axis, pairs)


def after(value, *others):
    return lax.optimization_barrier((value, *others))[0]


def all_after(values, *markers):
    return lax.optimization_barrier((*values, *markers))[: len(values)]


def send_rows(shard):
    if lax.axis_size("dp") != 8:
        return (lax.all_gather(shard, "dp", axis=0, tiled=True),)
    return tuple(swapped(shard, "dp", flip) for flip in (2, 4, 6))


def join_rows(shard, arrived):
    if len(arrived) == 1:
        return arrived
    side = jnp.concatenate([shard, *arrived], axis=0)
    return side, swapped(side, "dp", 1)


def added(*values):
    total = values[0].astype(F32)
    for value in values[1:]:
        total = total + value.astype(F32)
    return total


def sum_stages(pieces):
    if lax.axis_size("dp") != 8:
        shard = lax.psum_scatter(pieces[0], "dp", scatter_dimension=0, tiled=True)
        shard = lax.psum(shard, "pipe")
        (shard,) = yield (), (shard,)
        yield None, shard.astype(F32)
        return
    mine, theirs = pieces
    (other,) = yield (theirs,), (swapped(theirs, "dp", 1),)
    rows = mine.shape[0] // 4
    pair = []
    for step in range(4):
        part = slice(step * rows, (step + 1) * rows)
        pair.append(added(mine[part], other[part]).astype(BF16))
    arrived = yield pair, tuple(swapped(pair[step], "dp", 2 * step) for step in (1, 2, 3))
    shard = added(pair[0], *arrived).astype(BF16)
    flip = 1
    while flip < lax.axis_size("pipe"):
        (other,) = yield (shard,), (swapped(shard, "pipe", flip),)
        flip *= 2
        shard = added(shard, other)
        if flip < lax.axis_size("pipe"):
            shard = shard.astype(BF16)
    yield None, shard


def line_stages(shard):
    count = lax.axis_size("pipe")
    if count != 4:
        yield None, lax.psum(shard, "pipe").astype(F32)
        return
    (other,) = yield (shard,), (lax.ppermute(shard, "pipe", [(0, 1), (3, 2)]),)
    shard = added(shard, other).astype(BF16)
    (other,) = yield (shard,), (lax.ppermute(shard, "pipe", [(1, 2), (2, 1)]),)
    shard = added(shard, other).astype(BF16)
    (other,) = yield (shard,), (lax.ppermute(shard, "pipe", [(1, 0), (2, 3)]),)
    place = lax.axis_index("pipe")
    yield None, jnp.where((place == 0) | (place == 3), other, shard).astype(F32)


class Chunk:
    def __init__(self, terms, stages=sum_stages):
        self.stages = stages(terms)
        self.sent, self.result = next(self.stages)

    def step(self, *markers):
        if self.sent is None:
            return ()
        arrived = all_after(self.result, *markers) if markers else self.result
        self.sent, self.result = self.stages.send(arrived)
        return (self.result,) if self.sent is None else self.sent

    def finish(self):
        while self.sent is not None:
            self.step()
        return self.result


def local(
    fwd_latents,
    fwd_segments,
    stash_latents,
    stash_segments,
    upstream_grad,
    qkv_weight,
    out_weight,
    mlp_weight,
    norm_gain,
    biases,
):
    fwd_x, stash_x = fwd_latents[0], stash_latents[0]
    count, width = fwd_x.shape
    pieces = 2 if lax.axis_size("dp") == 8 else 1
    fwd_row, stash_row = fwd_segments, stash_segments
    fwd_col = stash_col = None
    own = norm_gain.shape[1]
    small = jnp.concatenate(
        [norm_gain, biases, jnp.zeros((PARAM_ROWS - 9, own), norm_gain.dtype)], axis=0
    )

    def qkv_shard(first, heads):
        cut = qkv_weight[:, :, first * HEAD : (first + heads) * HEAD]
        return jnp.concatenate([cut[0], cut[1], cut[2]], axis=1)

    first_shard = qkv_shard(*FORWARD_GROUPS[0])
    if pieces == 2:
        small = jnp.pad(small, ((0, 0), (0, first_shard.shape[1] - own)))
        first_shard = jnp.concatenate([first_shard, small], axis=0)
    qkv_shards = [first_shard] + [qkv_shard(*group) for group in FORWARD_GROUPS[1:]]
    flights = []
    for shard in qkv_shards:
        if flights:
            shard = after(shard, *flights[-1])
        flights.append(send_rows(shard))
    middle = jnp.concatenate([out_weight, mlp_weight[0]], axis=1)
    middle = (lax.all_gather(after(middle, *flights[0]), "dp", axis=0, tiled=True),)
    last = (lax.all_gather(mlp_weight[1], "dp", axis=0, tiled=True),)
    gathered = [join_rows(qkv_shards[0], flights[0])]
    if pieces == 1:
        params = lax.all_gather(small, "dp", axis=1, tiled=True)
    else:
        params = None
    half = count // 32 * 16
    upstream = upstream_grad[0]
    cotangent = [shifted(upstream[:half], "pipe", -1), shifted(upstream[half:], "pipe", -1)]

    saved, fwd_mixed = [], []
    normed = (stash_x, fwd_x)
    if params is not None:
        stash_col, fwd_col = (
            jnp.broadcast_to(row[0].astype(F32)[:, None], (count, 128)) for row in (stash_row, fwd_row)
        )
        plain = [normal_rows(rows.astype(F32))[0] for rows in normed]
        z_rows = plain[0].astype(BF16)
        normed = tuple(
            (rows * params[0:1].astype(F32) + params[2:3].astype(F32)).astype(BF16)
            for rows in plain
        )
    for index, (first, heads) in enumerate(FORWARD_GROUPS):
        (kept, plain), extra = attention_group(
            [(normed[0], stash_col, stash_row, True), (normed[1], fwd_col, fwd_row, False)],
            gathered[index], params, first, heads,
        )
        if extra:
            normed, (stash_col, fwd_col, z_rows, params) = tuple(extra[:2]), extra[2:]
        saved.append(kept)
        fwd_mixed.append(plain[0])
        here = ()
        if index:
            here = all_after((cotangent[index - 1],), plain[0])
            cotangent[index - 1] = here[0]
        if index + 1 < len(FORWARD_GROUPS):
            arrived = all_after(flights[index + 1], plain[0], *here)
            gathered.append(join_rows(qkv_shards[index + 1], arrived))
    stash_mixed = [group[3] for group in saved]
    dattended, dmixed, mlp_terms, *terms = middle_stash(
        stash_x, cotangent, stash_mixed, middle, last, params, stash_col, pieces
    )
    mlp_part = lax.psum_scatter(mlp_terms, "dp", scatter_dimension=0, tiled=True)
    running = [Chunk(terms)]

    def advance(marker):
        return [value for chunk in running for value in chunk.step(marker)]

    def begin(terms, sent):
        running.append(Chunk([*terms[:-1], after(terms[-1], *sent)]))
        return running[-1].step()

    result = mlp_fwd(
        after(fwd_x, dmixed), fwd_mixed, middle, last, params, fwd_col, (half, count - half)
    )
    latents = [shifted(rows, "pipe", 1) for rows in result]
    sent = advance(result[0])
    dprojected = []
    for index, (first, heads) in enumerate(BACKWARD_GROUPS):
        part, *terms = attention_backward(
            saved, after(dmixed, *sent), z_rows, first, heads, pieces
        )
        dprojected.append(part)
        sent = advance(part)
        if index < 2:
            (latents[index],) = all_after((latents[index],), part)
            sent.append(latents[index])
        if index == 1:
            (mlp_part,) = all_after((mlp_part,), part)
            mlp_total = lax.psum(mlp_part, "pipe")
            sent.append(mlp_part)
        sent += begin(terms, sent)
        dmixed = after(dmixed, part)
    input_grad, latents = input_backward(
        after(stash_x, *sent), dattended, dprojected, gathered, params, latents
    )
    newest, *older = running[::-1]
    sent = newest.step(input_grad)
    for chunk in older:
        sent = (*sent, *chunk.step(input_grad, *sent))
    sent = newest.step(*sent)
    (mlp_total,) = all_after((mlp_total,), input_grad, *sent)
    mlp_total = mlp_total.astype(F32)
    out_total, *qkv_totals = [chunk.finish() for chunk in running]

    rows = qkv_weight.shape[1]
    gain = norm_gain[0].astype(F32)[:, None]
    shift = biases[0].astype(F32)[:, None]
    grads, sums, gain_first, shift_first = [], [], 0.0, 0.0
    for kind in range(3):
        cut = [
            total[:, kind * total.shape[1] // 3 : (kind + 1) * total.shape[1] // 3]
            for total in qkv_totals
        ]
        cut = jnp.concatenate(cut, axis=1)
        weight = qkv_weight[kind].astype(F32)
        grads.append(gain * cut[:rows] + shift * cut[rows : rows + 1])
        sums.append(cut[rows : rows + 1])
        gain_first += jnp.sum(weight * cut[:rows], axis=1)
        shift_first += jnp.sum(weight * cut[rows : rows + 1], axis=1)
    place = lax.axis_index("dp") * rows

    def own_part(row):
        return lax.dynamic_slice_in_dim(row, place, rows, axis=row.ndim - 1)

    late = own_part(out_total[rows : rows + 5])
    gain_grad = jnp.stack([gain_first, late[0]])
    bias_grad = jnp.stack(
        [shift_first, own_part(sums[0][0]), own_part(sums[2][0]), late[2], late[1], late[3], late[4]]
    )
    return (
        latents[None],
        input_grad[None],
        jnp.stack(grads),
        out_total[:rows],
        jnp.stack([mlp_total[:, :width], mlp_total[:, width:]]),
        gain_grad,
        bias_grad,
        late[1],
    )


def solution(mesh):
    in_specs = (
        P("pipe", "dp", None),
        P("pipe", "dp"),
        P("pipe", "dp", None),
        P("pipe", "dp"),
        P("pipe", "dp", None),
        P(None, "dp", None),
        P("dp", None),
        P(None, "dp", None),
        P(None, "dp"),
        P(None, "dp"),
    )
    out_specs = (
        P("pipe", "dp", None),
        P("pipe", "dp", None),
        P(None, "dp", None),
        P("dp", None),
        P(None, "dp", None),
        P(None, "dp"),
        P(None, "dp"),
        P("dp"),
    )
    return jax.shard_map(local, mesh=mesh, in_specs=in_specs, out_specs=out_specs, check_vma=False)
```

```python
import functools

import jax
import jax.numpy as jnp
from jax import lax
from jax.experimental import pallas as pl
from jax.experimental.pallas import tpu as pltpu
from jax.sharding import PartitionSpec as P

HEADS = 8
HEAD = 128
EPSILON = 1e-05
SCALE = HEAD ** (-0.5)
LOG2E = 1.4426950408889634
GELU_C = 0.7978845608028654
GELU_A = 0.044715
FORWARD_GROUPS = ((0, 1), (1, 3), (4, 4))
BACKWARD_GROUPS = ((0, 3), (3, 3), (6, 2))
VMEM_LIMIT = 56 * 2**20
PARAM_ROWS = 16

F32 = jnp.float32
BF16 = jnp.bfloat16
ANY = pl.BlockSpec(memory_space=pl.ANY)
VMEM = pl.BlockSpec(memory_space=pltpu.VMEM)


def sds(shape, dtype=BF16):
    return jax.ShapeDtypeStruct(shape, dtype)


def dot_nn(a, b):
    return jnp.dot(a, b, preferred_element_type=F32)


def dot_nt(a, b):
    return lax.dot_general(a, b, (((1,), (1,)), ((), ())), preferred_element_type=F32)


def dot_tn(a, b):
    return lax.dot_general(a, b, (((0,), (0,)), ((), ())), preferred_element_type=F32)


class Mover:
    def __init__(self, sems):
        self.sems = sems
        self.used = 0
        self.open = []

    def start(self, source, target):
        copy = pltpu.make_async_copy(source, target, self.sems.at[self.used])
        self.used += 1
        copy.start()
        return copy

    def put(self, source, target):
        self.open.append(self.start(source, target))

    def finish(self):
        for copy in self.open:
            copy.wait()


def load_rows(move, pieces, target, columns=None, rows=None):
    columns = pl.ds(0, target.shape[1]) if columns is None else columns
    if len(pieces) == 1:
        return [move.start(pieces[0].at[pl.ds(0, target.shape[0]), columns], target)]
    mine = lax.axis_index("dp")
    step_rows = pieces[0].shape[0] // 4
    rows = step_rows if rows is None else rows
    copies = []
    for step in range(4):
        for side in range(2):
            owner = mine ^ (2 * step + side)
            source = pieces[side].at[pl.ds(step * step_rows, rows), columns]
            copies.append(
                move.start(source, target.at[pl.ds(pl.multiple_of(owner * rows, rows), rows)])
            )
    return copies


def load_side_by_side(move, refs, target):
    copies, place = [], 0
    for ref in refs:
        copies.append(move.start(ref, target.at[:, pl.ds(place, ref.shape[1])]))
        place += ref.shape[1]
    return copies


def store_terms(move, terms, left, right, pieces, extra):
    count = lax.axis_size("dp")
    rows = terms.shape[0] // count
    whole = rows + extra.shape[0]
    mine = lax.axis_index("dp")
    for index in range(0, count, 2):
        pair = index if len(pieces) == 1 else (mine ^ index) // 2 * 2
        start = pl.multiple_of(pair * rows, 2 * rows)
        block = pl.ds(start, 2 * rows)
        if 2 * rows % 128:
            if index == 0:
                terms[...] = dot_tn(left[...], right[...]).astype(BF16)
        else:
            terms[block, :] = dot_tn(left[:, block], right[...]).astype(BF16)
        for near in range(2):
            if len(pieces) == 1:
                owner, target, place = index + near, pieces[0], index + near
            else:
                owner, target, place = mine ^ (index + near), pieces[near], index // 2
            start = pl.multiple_of(owner * rows, rows)
            move.put(terms.at[pl.ds(start, rows)], target.at[pl.ds(place * whole, rows)])
            move.put(extra, target.at[pl.ds(place * whole + rows, extra.shape[0])])


def term_shapes(width, columns, sides):
    count = lax.axis_size("dp")
    return [sds(((width + count * PARAM_ROWS) // sides, columns))] * sides


def wait_all(copies):
    for copy in copies:
        copy.wait()


def tiles_of(count, size):
    return [pl.ds(start, min(size, count - start)) for start in range(0, count, size)]


def normal_rows(rows):
    centred = rows - jnp.mean(rows, axis=-1, keepdims=True)
    root = lax.rsqrt(jnp.mean(centred * centred, axis=-1, keepdims=True) + EPSILON)
    return centred * root, root


def column_sum(rows):
    return jnp.sum(rows, axis=0, keepdims=True)


def kernel_call(body, name, inputs, in_specs, outs, scratch, copies, flops):
    moved = sum(a.size * a.dtype.itemsize for a in inputs)
    moved += sum(int(jnp.dtype(o.dtype).itemsize) * functools.reduce(int.__mul__, o.shape) for o in outs)
    return pl.pallas_call(
        body,
        name=name,
        out_shape=outs,
        in_specs=in_specs,
        out_specs=[ANY] * len(outs),
        scratch_shapes=list(scratch) + [pltpu.SemaphoreType.DMA((copies,))],
        compiler_params=pltpu.CompilerParams(vmem_limit_bytes=VMEM_LIMIT),
        cost_estimate=pl.CostEstimate(flops=int(flops), bytes_accessed=int(moved), transcendentals=0),
    )(*inputs)


def load_params(move, pieces, rows, target):
    mine = lax.axis_index("dp")
    step_rows = pieces[0].shape[0] // 4
    width = target.shape[1] // 8
    copies = []
    for step in range(4):
        for side in range(2):
            owner = mine ^ (2 * step + side)
            copies.append(
                move.start(
                    pieces[side].at[pl.ds(step * step_rows + rows, PARAM_ROWS), pl.ds(0, width)],
                    target.at[:, pl.ds(pl.multiple_of(owner * width, width), width)],
                )
            )
    return copies


def attention_group(batches, weight, params, first_head, heads):
    count, width = batches[0][0].shape
    side = heads * HEAD
    pieces = len(weight)
    total = len(batches)
    tile = count // 4
    opening = params is None
    own_rows = width // 8 if pieces == 2 else width

    def body(*refs):
        each = 2 if opening else 3
        inputs = [refs[each * i : each * (i + 1)] for i in range(total)]
        w_refs = refs[each * total : each * total + pieces]
        at = each * total + pieces
        if not opening:
            p_ref = refs[at]
            at += 1
        outputs = []
        for _, _, _, keep in batches:
            outputs.append(refs[at : at + (6 if keep else 1)])
            at += 6 if keep else 1
        if opening:
            normed_outs = refs[at : at + total]
            col_outs = refs[at + total : at + 2 * total]
            z_out, p_out = refs[at + 2 * total : at + 2 * total + 2]
            at += 2 * total + 2
        params_v, w_v, *held = refs[at:-1]
        if opening:
            z_v, *held = held
        move = Mover(refs[-1])
        if not opening:
            loads = [move.start(p_ref, params_v)]
        else:
            loads = load_params(move, w_refs, own_rows, params_v)
        scratch, batch_loads = [], []
        for index, (_, _, _, keep) in enumerate(batches):
            scratch.append(held[: 9 if keep else 7])
            held = held[9 if keep else 7 :]
            normed_v, col_v, row_v = scratch[index][:3]
            batch_loads.append(move.start(inputs[index][0], normed_v))
            if index == 0:
                w_loads = load_rows(move, w_refs, w_v, rows=own_rows)
            ids = [move.start(inputs[index][1], row_v)]
            if not opening:
                ids.append(move.start(inputs[index][2], col_v))
            scratch[index] = (*scratch[index], ids)
        wait_all(loads)
        if opening:
            move.put(params_v, p_out)
        at = first_head * HEAD
        q_shift = params_v[3:4, at : at + side].astype(F32)
        v_shift = params_v[4:5, at : at + side].astype(F32)
        for index, (_, _, _, keep) in enumerate(batches):
            normed_v, col_v, row_v, q, k, v, o = scratch[index][:7]
            batch_loads[index].wait()
            if opening:
                gain = params_v[0:1, :].astype(F32)
                shift = params_v[2:3, :].astype(F32)
                for part in tiles_of(count, 208):
                    z, _ = normal_rows(normed_v[part, :].astype(F32))
                    normed_v[part, :] = (z * gain + shift).astype(BF16)
                    if keep:
                        z_v[part, :] = z.astype(BF16)
                move.put(normed_v, normed_outs[index])
                if keep:
                    move.put(z_v, z_out)
                wait_all(scratch[index][-1])
                top = lax.broadcasted_iota(jnp.int32, (16, count), 0) == 0
                spread = jnp.where(top, row_v[...].astype(F32), 0.0).astype(BF16)
                col_v[...] = dot_tn(spread, jnp.ones((16, 128), BF16))
                move.put(col_v, col_outs[index])
            if index == 0:
                wait_all(w_loads)
            for part in tiles_of(count, count):
                projected = dot_nn(normed_v[part, :], w_v[...])
                q[part, :] = (projected[:, :side] + q_shift).astype(BF16)
                k[part, :] = projected[:, side : 2 * side].astype(BF16)
                v[part, :] = (projected[:, 2 * side :] + v_shift).astype(BF16)
            if keep:
                q_out, k_out, v_out, o_out, e_out, l_out = outputs[index]
                e_all, inv = scratch[index][7:9]
                move.put(q, q_out)
                move.put(k, k_out)
                move.put(v, v_out)
            else:
                o_out = outputs[index][0]
            if not opening:
                wait_all(scratch[index][-1])
            row = row_v[...].astype(F32)
            for head in range(heads):
                lanes = pl.ds(head * HEAD, HEAD)
                key_rows = k[:, lanes]
                value_rows = v[:, lanes]
                wide = jnp.concatenate([value_rows, jnp.ones_like(value_rows)], axis=1)
                for part in tiles_of(count, tile):
                    scores = dot_nt(q[part, lanes], key_rows)
                    scores = jnp.where(col_v[part, 0:1] == row, scores, -1e30)
                    top = jnp.max(scores, axis=1, keepdims=True)
                    e = jnp.exp2(scores * (SCALE * LOG2E) - top * (SCALE * LOG2E)).astype(BF16)
                    if keep:
                        e_all[head, part, :] = e
                    both = dot_nn(e, wide)
                    inverse = 1.0 / both[:, HEAD:]
                    if keep:
                        inv[part, lanes] = inverse
                    o[part, lanes] = (both[:, :HEAD] * inverse).astype(BF16)
                if keep:
                    move.put(e_all.at[head], e_out.at[head])
            move.put(o, o_out)
            if keep:
                move.put(inv, l_out)
        move.finish()

    buf = pltpu.VMEM((count, side), BF16)
    scratch = [pltpu.VMEM((PARAM_ROWS, width), BF16), pltpu.VMEM((width, 3 * side), BF16)]
    scratch += [pltpu.VMEM((count, width), BF16)] if opening else []
    outs, inputs = [], []
    for normed, ids_col, ids_row, keep in batches:
        inputs += [normed, ids_row] if opening else [normed, ids_row, ids_col]
        scratch += [
            pltpu.VMEM((count, width), BF16), pltpu.VMEM((count, 128), F32),
            pltpu.VMEM(ids_row.shape, jnp.int32), buf, buf, buf, buf,
        ]
        outs += [sds((count, side))]
        if keep:
            scratch += [pltpu.VMEM((heads, count, count), BF16), pltpu.VMEM((count, side), F32)]
            outs += [sds((count, side))] * 3 + [sds((heads, count, count)), sds((count, side), F32)]
    if opening:
        outs += [sds((count, width))] * total + [sds((count, 128), F32)] * total
        outs += [sds((count, width)), sds((PARAM_ROWS, width))]
    flops = total * (2 * count * width * 3 * side + 8 * heads * count * count * HEAD)
    result = kernel_call(
        body, f"attention_{'_'.join('stash' if b[3] else 'fwd' for b in batches)}_{first_head}",
        (*inputs, *weight, *([] if opening else [params])),
        [ANY] * ((2 if opening else 3) * total + pieces + (0 if opening else 1)), outs, scratch,
        19 + total * (5 + 5 + heads), flops,
    )
    split = []
    for _, _, _, keep in batches:
        split.append(result[: 6 if keep else 1])
        result = result[6 if keep else 1 :]
    return split, result


def gelu_parts(hidden):
    square = hidden * hidden
    bend = jnp.tanh(GELU_C * hidden * (1.0 + GELU_A * square))
    half = 0.5 * (1.0 + bend)
    slope = half + 0.5 * hidden * (1.0 - bend * bend) * (GELU_C * (1.0 + 3.0 * GELU_A * square))
    return hidden * half, slope


def mlp_fwd(latents, mixed, weight, last, params, ids_col, cuts):
    count, width = latents.shape
    split = len(mixed)
    tile = count // 4

    def body(*refs):
        x_ref = refs[0]
        m_refs = refs[1 : 1 + split]
        w_ref, l_ref = refs[1 + split : 3 + split]
        p_ref, col_ref = refs[1 + split + 2 : 3 + split + 2]
        y_outs = refs[3 + split + 2 : 3 + split + 2 + len(cuts)]
        x, mixed_v, w, w_last, p, col, rest, n, y, sems = refs[3 + split + 2 + len(cuts) :]
        move = Mover(sems)
        loads = [move.start(p_ref, p), move.start(x_ref, x)]
        loads += load_side_by_side(move, m_refs, mixed_v)
        loads.append(move.start(w_ref, w.at[0]))
        load_next = [move.start(l_ref.at[0], w.at[1])]
        load_last = [move.start(l_ref.at[1], w_last), move.start(col_ref, col)]
        wait_all(loads)
        rows = [p[i : i + 1, :].astype(F32) for i in range(9)]
        for part in tiles_of(count, tile):
            attended = x[part, :].astype(F32) + dot_nn(mixed_v[part, :], w[0]) + rows[5]
            rest[part, :] = attended
            z, _ = normal_rows(attended)
            n[part, :] = (z * rows[1] + rows[6]).astype(BF16)
        wait_all(load_next)
        for index, part in enumerate(tiles_of(count, tile)):
            hidden = dot_nn(n[part, :], w[1]) + rows[7]
            active = gelu_parts(hidden)[0].astype(BF16)
            if index == 0:
                wait_all(load_last)
            result = rest[part, :] + dot_nn(active, w_last[...]) + rows[8]
            y[part, :] = jnp.where(col[part, 0:1] < 3, result, 0.0).astype(BF16)
        place = 0
        for out in y_outs:
            move.put(y.at[pl.ds(place, out.shape[0])], out)
            place += out.shape[0]
        move.finish()

    buf = pltpu.VMEM((count, width), BF16)
    return kernel_call(
        body, "mlp_fwd", (latents, *mixed, weight, last, params, ids_col),
        [ANY] * (3 + split + 2),
        [sds((rows, width)) for rows in cuts],
        [buf, buf, pltpu.VMEM((2, width, width), BF16), pltpu.VMEM((width, width), BF16),
         pltpu.VMEM(params.shape, BF16), pltpu.VMEM(ids_col.shape, F32),
         pltpu.VMEM((count, width), F32), buf, buf],
        3 + split + 24 + len(cuts), 6 * count * width * width,
    )


def middle_stash(latents, arrived, mixed, weight, last, params, ids_col, sides):
    count, width = latents.shape
    split = len(mixed)
    tile = count // 4
    wide = width // 4

    def body(*refs):
        g_refs, refs = refs[: len(arrived)], refs[len(arrived) - 1 :]
        x_ref = refs[1]
        m_refs = refs[2 : 2 + split]
        w_ref, l_ref = refs[2 + split : 4 + split]
        p_ref, col_ref, d_out, m_out, t_out = refs[2 + split + 2 : 7 + split + 2]
        grads = refs[7 + split + 2 : 7 + split + 2 + sides]
        (x, cot, mixed_v, w, w_last, p, col, n, z_v, r_v, act, slope_v, dhid, datt, dattn, dmix,
         terms, out_terms, sums, extra, sems) = refs[7 + split + 2 + sides :]
        move = Mover(sems)
        loads = [move.start(p_ref, p), move.start(x_ref, x)]
        loads += load_side_by_side(move, m_refs, mixed_v)
        loads.append(move.start(w_ref, w.at[0]))
        load_next = [move.start(l_ref.at[0], w.at[1])]
        load_back, place = [move.start(col_ref, col)], 0
        for ref in g_refs:
            load_back.append(move.start(ref, cot.at[pl.ds(place, ref.shape[0])]))
            place += ref.shape[0]
        load_last = [move.start(l_ref.at[1], w_last)]
        wait_all(loads)
        rows = [p[i : i + 1, :].astype(F32) for i in range(9)]
        for index, part in enumerate(tiles_of(count, tile)):
            attended = x[part, :].astype(F32) + dot_nn(mixed_v[part, :], w[0]) + rows[5]
            z, root = normal_rows(attended)
            z_v[part, :] = z.astype(BF16)
            r_v[part, :] = jnp.broadcast_to(root, (tile, 128))
            n[part, :] = (z * rows[1] + rows[6]).astype(BF16)
            if index == 0:
                wait_all(load_next)
            hidden = dot_nn(n[part, :], w[1]) + rows[7]
            active, slope = gelu_parts(hidden)
            act[part, :] = active.astype(BF16)
            slope_v[part, :] = slope.astype(BF16)
        wait_all(load_back)
        cot[...] = jnp.where(col[:, 0:1] < 3, cot[...].astype(F32), 0.0).astype(BF16)
        wait_all(load_last)
        totals = [jnp.zeros((1, width), F32) for _ in range(5)]
        for index, part in enumerate(tiles_of(count, tile)):
            dactive = dot_nt(cot[part, :], w_last[...])
            held = (slope_v[part, :].astype(F32) * dactive).astype(BF16)
            dhid[part, :] = held
            totals[3] += column_sum(held.astype(F32))
            totals[4] += column_sum(cot[part, :].astype(F32))
            block = pl.ds(index * wide, wide)
            terms[block, width:] = dot_tn(act[:, block], cot[...]).astype(BF16)
        move.put(terms.at[:, pl.ds(width, width)], t_out.at[:, pl.ds(width, width)])
        for index, part in enumerate(tiles_of(count, tile)):
            dnormed = dot_nt(dhid[part, :], w[1])
            z = z_v[part, :].astype(F32)
            totals[0] += column_sum(dnormed * z)
            totals[1] += column_sum(dnormed)
            dz = dnormed * rows[1]
            inner = dz - jnp.mean(dz, axis=-1, keepdims=True)
            inner = inner - z * jnp.mean(dz * z, axis=-1, keepdims=True)
            dattended = cot[part, :].astype(F32) + r_v[part, 0:1] * inner
            datt[part, :] = dattended
            held = dattended.astype(BF16)
            dattn[part, :] = held
            totals[2] += column_sum(held.astype(F32))
            block = pl.ds(index * wide, wide)
            terms[block, :width] = dot_tn(n[:, block], dhid[...]).astype(BF16)
            dmix[part, :] = dot_nt(held, w[0]).astype(BF16)
            move.put(datt.at[part], d_out.at[part])
            move.put(dmix.at[part], m_out.at[part])
        move.put(terms.at[:, pl.ds(0, width)], t_out.at[:, pl.ds(0, width)])
        for index in range(5):
            sums[index : index + 1, :] = totals[index]
        sums[5:PARAM_ROWS, :] = jnp.zeros((PARAM_ROWS - 5, width), F32)
        extra[...] = sums[...].astype(BF16)
        store_terms(move, out_terms, mixed_v, dattn, grads, extra)
        move.finish()

    buf = pltpu.VMEM((count, width), BF16)
    square = pltpu.VMEM((width, width), BF16)
    return kernel_call(
        body, "middle_stash", (*arrived, latents, *mixed, weight, last, params, ids_col),
        [ANY] * (3 + len(arrived) + split + 2),
        [sds((count, width), F32), sds((count, width)), sds((width, 2 * width))]
        + term_shapes(width, width, sides),
        [buf, buf, buf, pltpu.VMEM((2, width, width), BF16), square, pltpu.VMEM(params.shape, BF16),
         pltpu.VMEM(ids_col.shape, F32), buf, buf, pltpu.VMEM((count, 128), F32), buf, buf, buf,
         pltpu.VMEM((count, width), F32), buf, buf, pltpu.VMEM((width, 2 * width), BF16), square,
         pltpu.VMEM((PARAM_ROWS, width), F32), pltpu.VMEM((PARAM_ROWS, width), BF16)],
        3 + len(arrived) + split + 24 + 8 + 2 + 2 * lax.axis_size("dp"), 16 * count * width * width,
    )


def attention_backward(saved, dmixed, z_rows, first_head, heads, sides):
    count, width = z_rows.shape
    side = heads * HEAD
    tile = count // 2
    cuts, at = [], 0
    for index, arrays in enumerate(saved):
        own = arrays[0].shape[1] // HEAD
        low, high = max(first_head, at), min(first_head + heads, at + own)
        if low < high:
            cuts.append((index, low - at, low - first_head, high - low))
        at += own
    saved = [saved[cut[0]] for cut in cuts]
    groups = len(saved)

    def body(*refs):
        inputs = [refs[6 * i : 6 * i + 6] for i in range(groups)]
        m_ref, n_ref, d_out = refs[6 * groups : 6 * groups + 3]
        grads = refs[6 * groups + 3 : 6 * groups + 3 + sides]
        q, k, v, o, e, inv, dmix, n, dqkv, dscore, terms, sums, extra, sems = refs[
            6 * groups + 3 + sides :
        ]
        move = Mover(sems)
        load_m = move.start(m_ref.at[:, pl.ds(first_head * HEAD, side)], dmix)
        small, large = [], []
        for (q_ref, k_ref, v_ref, o_ref, e_ref, l_ref), cut in zip(inputs, cuts, strict=True):
            _, low, place, own = cut
            for head in range(own):
                source = pl.ds((low + head) * HEAD, HEAD)
                lanes = pl.ds((place + head) * HEAD, HEAD)
                small.append(
                    [
                        move.start(ref.at[:, source], target.at[:, lanes])
                        for ref, target in ((l_ref, inv), (o_ref, o), (v_ref, v))
                    ]
                )
                large.append(move.start(e_ref.at[low + head], e.at[place + head]))
                small[-1] += [
                    move.start(ref.at[:, source], target.at[:, lanes])
                    for ref, target in ((k_ref, k), (q_ref, q))
                ]
        load_n = move.start(n_ref, n)
        load_m.wait()
        for head in range(heads):
            lanes = pl.ds(head * HEAD, HEAD)
            wait_all(small[head])
            scaled = (dmix[:, lanes].astype(F32) * inv[:, lanes]).astype(BF16)
            row_sum = jnp.sum(scaled.astype(F32) * o[:, lanes].astype(F32), axis=1, keepdims=True)
            value_rows = v[:, lanes]
            head_keys = k[:, lanes]
            large[head].wait()
            for start in range(0, count, tile):
                part = pl.ds(start, tile)
                dprobs = dot_nt(scaled[start : start + tile], value_rows)
                held = e[head, part, :].astype(F32) * (dprobs - row_sum[start : start + tile])
                held = held.astype(BF16)
                dscore[part, :] = held
                dqkv[part, lanes] = (dot_nn(held, head_keys) * SCALE).astype(BF16)
            dqkv[:, pl.ds(side + head * HEAD, HEAD)] = (
                dot_tn(dscore[...], q[:, lanes]) * SCALE
            ).astype(BF16)
            dqkv[:, pl.ds(2 * side + head * HEAD, HEAD)] = dot_tn(e[head], scaled).astype(BF16)
        move.put(dqkv, d_out)
        sums[0:1, :] = column_sum(dqkv[...].astype(F32))
        sums[1:PARAM_ROWS, :] = jnp.zeros((PARAM_ROWS - 1, 3 * side), F32)
        extra[...] = sums[...].astype(BF16)
        load_n.wait()
        store_terms(move, terms, n, dqkv, grads, extra)
        move.finish()

    buf = pltpu.VMEM((count, side), BF16)
    return kernel_call(
        body, f"attention_backward_{first_head}",
        (*[array for group in saved for array in group], dmixed, z_rows),
        [ANY] * (6 * groups + 2),
        [sds((count, 3 * side))] + term_shapes(width, 3 * side, sides),
        [buf, buf, buf, buf, pltpu.VMEM((heads, count, count), BF16), pltpu.VMEM((count, side), F32),
         buf, pltpu.VMEM((count, width), BF16), pltpu.VMEM((count, 3 * side), BF16),
         pltpu.VMEM((count, count), BF16), pltpu.VMEM((width, 3 * side), BF16),
         pltpu.VMEM((PARAM_ROWS, 3 * side), F32), pltpu.VMEM((PARAM_ROWS, 3 * side), BF16)],
        3 + 6 * heads + 2 * lax.axis_size("dp"), 2 * count * width * 3 * side + 16 * heads * count * count * HEAD,
    )


def input_backward(latents, dattended, parts, weights, params, results):
    count, width = latents.shape
    pieces = len(weights[0])
    groups = len(parts)
    total = len(weights)
    tile = count // 4

    def body(*refs):
        x_ref, d_ref = refs[:2]
        g_refs = refs[2 : 2 + groups]
        at = 2 + groups
        w_refs = [refs[at + i * pieces : at + (i + 1) * pieces] for i in range(total)]
        at += total * pieces
        r_refs = refs[at : at + len(results)]
        at += len(results)
        p_ref, y_out, r_out, x, datt, dqkv, w, acc, y, r_v, p, sems = refs[at:]
        move = Mover(sems)
        loads = []
        for kind in range(3):
            own_loads = []
            place = 0
            for ref in g_refs:
                own = ref.shape[1] // 3
                own_loads.append(
                    move.start(ref.at[:, pl.ds(kind * own, own)], dqkv.at[kind, :, pl.ds(place, own)])
                )
                place += own
            place = 0
            for ref in w_refs:
                own = ref[0].shape[1] // 3
                own_loads += load_rows(
                    move, ref, w.at[kind, :, pl.ds(place, own)], pl.ds(kind * own, own), width // 8
                )
                place += own
            loads.append(own_loads)
        late = [move.start(x_ref, x), move.start(d_ref, datt), move.start(p_ref, p)]
        back, place = [], 0
        for ref in r_refs:
            back.append(move.start(ref, r_v.at[pl.ds(place, ref.shape[0])]))
            place += ref.shape[0]
        for kind in range(2):
            wait_all(loads[kind])
            for part in tiles_of(count, tile):
                dnormed = dot_nt(dqkv[kind, part, :], w[kind])
                acc[part, :] = dnormed if kind == 0 else acc[part, :] + dnormed
        wait_all(loads[2] + late)
        gain = p[0:1, :].astype(F32)
        for part in tiles_of(count, tile):
            dnormed = acc[part, :] + dot_nt(dqkv[2, part, :], w[2])
            z, root = normal_rows(x[part, :].astype(F32))
            dz = dnormed * gain
            inner = dz - jnp.mean(dz, axis=-1, keepdims=True)
            inner = inner - z * jnp.mean(dz * z, axis=-1, keepdims=True)
            y[part, :] = (datt[part, :] + root * inner).astype(BF16)
            move.put(y.at[part], y_out.at[part])
        wait_all(back)
        move.put(r_v, r_out)
        move.finish()

    buf = pltpu.VMEM((count, width), BF16)
    return kernel_call(
        body, "input_backward",
        (latents, dattended, *parts, *[piece for weight in weights for piece in weight], *results,
         params),
        [ANY] * (3 + groups + total * pieces + len(results)),
        [sds((count, width)), sds((count, width))],
        [buf, pltpu.VMEM((count, width), F32), pltpu.VMEM((3, count, width), BF16),
         pltpu.VMEM((3, width, width), BF16), pltpu.VMEM((count, width), F32), buf, buf,
         pltpu.VMEM(params.shape, BF16)],
        3 + 3 * groups + 24 * total + len(results) + 5, 6 * count * width * width,
    )


def swapped(value, axis, flip):
    count = lax.axis_size(axis)
    return lax.ppermute(value, axis, [(source, source ^ flip) for source in range(count)])


def shifted(value, axis, steps):
    count = lax.axis_size(axis)
    pairs = [(source, (source + steps) % count) for source in range(count)]
    return lax.ppermute(value, axis, pairs)


def after(value, *others):
    return lax.optimization_barrier((value, *others))[0]


def all_after(values, *markers):
    return lax.optimization_barrier((*values, *markers))[: len(values)]


def send_rows(shard):
    if lax.axis_size("dp") != 8:
        return (lax.all_gather(shard, "dp", axis=0, tiled=True),)
    return tuple(swapped(shard, "dp", flip) for flip in (2, 4, 6))


def join_rows(shard, arrived):
    if len(arrived) == 1:
        return arrived
    side = jnp.concatenate([shard, *arrived], axis=0)
    return side, swapped(side, "dp", 1)


def added(*values):
    total = values[0].astype(F32)
    for value in values[1:]:
        total = total + value.astype(F32)
    return total


def sum_stages(pieces):
    if lax.axis_size("dp") != 8:
        shard = lax.psum_scatter(pieces[0], "dp", scatter_dimension=0, tiled=True)
        shard = lax.psum(shard, "pipe")
        (shard,) = yield (), (shard,)
        yield None, shard.astype(F32)
        return
    mine, theirs = pieces
    (other,) = yield (theirs,), (swapped(theirs, "dp", 1),)
    rows = mine.shape[0] // 4
    pair = []
    for step in range(4):
        part = slice(step * rows, (step + 1) * rows)
        pair.append(added(mine[part], other[part]).astype(BF16))
    arrived = yield pair, tuple(swapped(pair[step], "dp", 2 * step) for step in (1, 2, 3))
    shard = added(pair[0], *arrived).astype(BF16)
    flip = 1
    while flip < lax.axis_size("pipe"):
        (other,) = yield (shard,), (swapped(shard, "pipe", flip),)
        flip *= 2
        shard = added(shard, other)
        if flip < lax.axis_size("pipe"):
            shard = shard.astype(BF16)
    yield None, shard


def line_stages(shard):
    count = lax.axis_size("pipe")
    if count != 4:
        yield None, lax.psum(shard, "pipe").astype(F32)
        return
    (other,) = yield (shard,), (lax.ppermute(shard, "pipe", [(0, 1), (3, 2)]),)
    shard = added(shard, other).astype(BF16)
    (other,) = yield (shard,), (lax.ppermute(shard, "pipe", [(1, 2), (2, 1)]),)
    shard = added(shard, other).astype(BF16)
    (other,) = yield (shard,), (lax.ppermute(shard, "pipe", [(1, 0), (2, 3)]),)
    place = lax.axis_index("pipe")
    yield None, jnp.where((place == 0) | (place == 3), other, shard).astype(F32)


class Chunk:
    def __init__(self, terms, stages=sum_stages):
        self.stages = stages(terms)
        self.sent, self.result = next(self.stages)

    def step(self, *markers):
        if self.sent is None:
            return ()
        arrived = all_after(self.result, *markers) if markers else self.result
        self.sent, self.result = self.stages.send(arrived)
        return (self.result,) if self.sent is None else self.sent

    def finish(self):
        while self.sent is not None:
            self.step()
        return self.result


def local(
    fwd_latents,
    fwd_segments,
    stash_latents,
    stash_segments,
    upstream_grad,
    qkv_weight,
    out_weight,
    mlp_weight,
    norm_gain,
    biases,
):
    fwd_x, stash_x = fwd_latents[0], stash_latents[0]
    count, width = fwd_x.shape
    pieces = 2 if lax.axis_size("dp") == 8 else 1
    fwd_row, stash_row = fwd_segments, stash_segments
    fwd_col = stash_col = None
    own = norm_gain.shape[1]
    small = jnp.concatenate(
        [norm_gain, biases, jnp.zeros((PARAM_ROWS - 9, own), norm_gain.dtype)], axis=0
    )

    def qkv_shard(first, heads):
        cut = qkv_weight[:, :, first * HEAD : (first + heads) * HEAD]
        return jnp.concatenate([cut[0], cut[1], cut[2]], axis=1)

    first_shard = qkv_shard(*FORWARD_GROUPS[0])
    if pieces == 2:
        small = jnp.pad(small, ((0, 0), (0, first_shard.shape[1] - own)))
        first_shard = jnp.concatenate([first_shard, small], axis=0)
    qkv_shards = [first_shard] + [qkv_shard(*group) for group in FORWARD_GROUPS[1:]]
    flights = []
    for shard in qkv_shards:
        if flights:
            shard = after(shard, *flights[-1])
        flights.append(send_rows(shard))
    middle = jnp.concatenate([out_weight, mlp_weight[0]], axis=1)
    middle = (lax.all_gather(after(middle, *flights[0]), "dp", axis=0, tiled=True),)
    middle = lax.all_gather(after(out_weight, first_shard), "dp", axis=0, tiled=True)
    last = lax.all_gather(after(mlp_weight, first_shard), "dp", axis=1, tiled=True)
    gathered = [join_rows(qkv_shards[0], flights[0])]
    if pieces == 1:
        params = lax.all_gather(small, "dp", axis=1, tiled=True)
    else:
        params = None
    half = count // 32 * 16
    upstream = upstream_grad[0]
    cotangent = [shifted(upstream[:half], "pipe", -1), shifted(upstream[half:], "pipe", -1)]

    saved, fwd_mixed = [], []
    normed = (stash_x, fwd_x)
    if params is not None:
        stash_col, fwd_col = (
            jnp.broadcast_to(row[0].astype(F32)[:, None], (count, 128)) for row in (stash_row, fwd_row)
        )
        plain = [normal_rows(rows.astype(F32))[0] for rows in normed]
        z_rows = plain[0].astype(BF16)
        normed = tuple(
            (rows * params[0:1].astype(F32) + params[2:3].astype(F32)).astype(BF16)
            for rows in plain
        )
    for index, (first, heads) in enumerate(FORWARD_GROUPS):
        (kept, plain), extra = attention_group(
            [(normed[0], stash_col, stash_row, True), (normed[1], fwd_col, fwd_row, False)],
            gathered[index], params, first, heads,
        )
        if extra:
            normed, (stash_col, fwd_col, z_rows, params) = tuple(extra[:2]), extra[2:]
        saved.append(kept)
        fwd_mixed.append(plain[0])
        here = ()
        if index:
            here = all_after((cotangent[index - 1],), plain[0])
            cotangent[index - 1] = here[0]
        if index + 1 < len(FORWARD_GROUPS):
            arrived = all_after(flights[index + 1], plain[0], *here)
            gathered.append(join_rows(qkv_shards[index + 1], arrived))
    stash_mixed = [group[3] for group in saved]
    dattended, dmixed, mlp_terms, *terms = middle_stash(
        stash_x, cotangent, stash_mixed, middle, last, params, stash_col, pieces
    )
    mlp_part = lax.psum_scatter(mlp_terms, "dp", scatter_dimension=0, tiled=True)
    running = [Chunk(terms)]

    def advance(marker):
        return [value for chunk in running for value in chunk.step(marker)]

    def begin(terms, sent):
        running.append(Chunk([*terms[:-1], after(terms[-1], *sent)]))
        return running[-1].step()

    result = mlp_fwd(
        after(fwd_x, dmixed), fwd_mixed, middle, last, params, fwd_col, (half, count - half)
    )
    latents = [shifted(rows, "pipe", 1) for rows in result]
    sent = advance(result[0])
    dprojected = []
    for index, (first, heads) in enumerate(BACKWARD_GROUPS):
        part, *terms = attention_backward(
            saved, after(dmixed, *sent), z_rows, first, heads, pieces
        )
        dprojected.append(part)
        sent = advance(part)
        if index < 2:
            (latents[index],) = all_after((latents[index],), part)
            sent.append(latents[index])
        if index == 1:
            (mlp_part,) = all_after((mlp_part,), part)
            mlp_total = lax.psum(mlp_part, "pipe")
            sent.append(mlp_part)
        sent += begin(terms, sent)
        dmixed = after(dmixed, part)
    input_grad, latents = input_backward(
        after(stash_x, *sent), dattended, dprojected, gathered, params, latents
    )
    newest, *older = running[::-1]
    sent = newest.step(input_grad)
    for chunk in older:
        sent = (*sent, *chunk.step(input_grad, *sent))
    sent = newest.step(*sent)
    (mlp_total,) = all_after((mlp_total,), input_grad, *sent)
    mlp_total = mlp_total.astype(F32)
    out_total, *qkv_totals = [chunk.finish() for chunk in running]

    out_total, norm_gain, biases = all_after((out_total, norm_gain, biases), *sent)
    rows = qkv_weight.shape[1]
    gain = norm_gain[0].astype(F32)[:, None]
    shift = biases[0].astype(F32)[:, None]
    grads, sums, gain_first, shift_first = [], [], 0.0, 0.0
    for kind in range(3):
        cut = [
            total[:, kind * total.shape[1] // 3 : (kind + 1) * total.shape[1] // 3]
            for total in qkv_totals
        ]
        cut = jnp.concatenate(cut, axis=1)
        weight = qkv_weight[kind].astype(F32)
        grads.append(gain * cut[:rows] + shift * cut[rows : rows + 1])
        sums.append(cut[rows : rows + 1])
        gain_first += jnp.sum(weight * cut[:rows], axis=1)
        shift_first += jnp.sum(weight * cut[rows : rows + 1], axis=1)
    place = lax.axis_index("dp") * rows

    def own_part(row):
        return lax.dynamic_slice_in_dim(row, place, rows, axis=row.ndim - 1)

    late = own_part(out_total[rows : rows + 5])
    gain_grad = jnp.stack([gain_first, late[0]])
    bias_grad = jnp.stack(
        [shift_first, own_part(sums[0][0]), own_part(sums[2][0]), late[2], late[1], late[3], late[4]]
    )
    return (
        latents[None],
        input_grad[None],
        jnp.stack(grads),
        out_total[:rows],
        jnp.stack([mlp_total[:, :width], mlp_total[:, width:]]),
        gain_grad,
        bias_grad,
        late[1],
    )


def solution(mesh):
    in_specs = (
        P("pipe", "dp", None),
        P("pipe", "dp"),
        P("pipe", "dp", None),
        P("pipe", "dp"),
        P("pipe", "dp", None),
        P(None, "dp", None),
        P("dp", None),
        P(None, "dp", None),
        P(None, "dp"),
        P(None, "dp"),
    )
    out_specs = (
        P("pipe", "dp", None),
        P("pipe", "dp", None),
        P(None, "dp", None),
        P("dp", None),
        P(None, "dp", None),
        P(None, "dp"),
        P(None, "dp"),
        P("dp"),
    )
    return jax.shard_map(local, mesh=mesh, in_specs=in_specs, out_specs=out_specs, check_vma=False)
```

```python
import functools

import jax
import jax.numpy as jnp
from jax import lax
from jax.experimental import pallas as pl
from jax.experimental.pallas import tpu as pltpu
from jax.sharding import PartitionSpec as P

HEADS = 8
HEAD = 128
EPSILON = 1e-05
SCALE = HEAD ** (-0.5)
LOG2E = 1.4426950408889634
GELU_C = 0.7978845608028654
GELU_A = 0.044715
FORWARD_GROUPS = ((0, 1), (1, 3), (4, 4))
BACKWARD_GROUPS = ((0, 3), (3, 3), (6, 2))
VMEM_LIMIT = 56 * 2**20
PARAM_ROWS = 16

F32 = jnp.float32
BF16 = jnp.bfloat16
ANY = pl.BlockSpec(memory_space=pl.ANY)
VMEM = pl.BlockSpec(memory_space=pltpu.VMEM)


def sds(shape, dtype=BF16):
    return jax.ShapeDtypeStruct(shape, dtype)


def dot_nn(a, b):
    return jnp.dot(a, b, preferred_element_type=F32)


def dot_nt(a, b):
    return lax.dot_general(a, b, (((1,), (1,)), ((), ())), preferred_element_type=F32)


def dot_tn(a, b):
    return lax.dot_general(a, b, (((0,), (0,)), ((), ())), preferred_element_type=F32)


class Mover:
    def __init__(self, sems):
        self.sems = sems
        self.used = 0
        self.open = []

    def start(self, source, target):
        copy = pltpu.make_async_copy(source, target, self.sems.at[self.used])
        self.used += 1
        copy.start()
        return copy

    def put(self, source, target):
        self.open.append(self.start(source, target))

    def finish(self):
        for copy in self.open:
            copy.wait()


def load_rows(move, pieces, target, columns=None, rows=None):
    columns = pl.ds(0, target.shape[1]) if columns is None else columns
    if len(pieces) == 1:
        return [move.start(pieces[0].at[pl.ds(0, target.shape[0]), columns], target)]
    mine = lax.axis_index("dp")
    step_rows = pieces[0].shape[0] // 4
    rows = step_rows if rows is None else rows
    copies = []
    for step in range(4):
        for side in range(2):
            owner = mine ^ (2 * step + side)
            source = pieces[side].at[pl.ds(step * step_rows, rows), columns]
            copies.append(
                move.start(source, target.at[pl.ds(pl.multiple_of(owner * rows, rows), rows)])
            )
    return copies


def load_side_by_side(move, refs, target):
    copies, place = [], 0
    for ref in refs:
        copies.append(move.start(ref, target.at[:, pl.ds(place, ref.shape[1])]))
        place += ref.shape[1]
    return copies


def store_terms(move, terms, left, right, pieces, extra):
    count = lax.axis_size("dp")
    rows = terms.shape[0] // count
    whole = rows + extra.shape[0]
    mine = lax.axis_index("dp")
    for index in range(0, count, 2):
        pair = index if len(pieces) == 1 else (mine ^ index) // 2 * 2
        start = pl.multiple_of(pair * rows, 2 * rows)
        block = pl.ds(start, 2 * rows)
        if 2 * rows % 128:
            if index == 0:
                terms[...] = dot_tn(left[...], right[...]).astype(BF16)
        else:
            terms[block, :] = dot_tn(left[:, block], right[...]).astype(BF16)
        for near in range(2):
            if len(pieces) == 1:
                owner, target, place = index + near, pieces[0], index + near
            else:
                owner, target, place = mine ^ (index + near), pieces[near], index // 2
            start = pl.multiple_of(owner * rows, rows)
            move.put(terms.at[pl.ds(start, rows)], target.at[pl.ds(place * whole, rows)])
            move.put(extra, target.at[pl.ds(place * whole + rows, extra.shape[0])])


def term_shapes(width, columns, sides):
    count = lax.axis_size("dp")
    return [sds(((width + count * PARAM_ROWS) // sides, columns))] * sides


def wait_all(copies):
    for copy in copies:
        copy.wait()


def tiles_of(count, size):
    return [pl.ds(start, min(size, count - start)) for start in range(0, count, size)]


def normal_rows(rows):
    centred = rows - jnp.mean(rows, axis=-1, keepdims=True)
    root = lax.rsqrt(jnp.mean(centred * centred, axis=-1, keepdims=True) + EPSILON)
    return centred * root, root


def column_sum(rows):
    return jnp.sum(rows, axis=0, keepdims=True)


def kernel_call(body, name, inputs, in_specs, outs, scratch, copies, flops):
    moved = sum(a.size * a.dtype.itemsize for a in inputs)
    moved += sum(int(jnp.dtype(o.dtype).itemsize) * functools.reduce(int.__mul__, o.shape) for o in outs)
    return pl.pallas_call(
        body,
        name=name,
        out_shape=outs,
        in_specs=in_specs,
        out_specs=[ANY] * len(outs),
        scratch_shapes=list(scratch) + [pltpu.SemaphoreType.DMA((copies,))],
        compiler_params=pltpu.CompilerParams(vmem_limit_bytes=VMEM_LIMIT),
        cost_estimate=pl.CostEstimate(flops=int(flops), bytes_accessed=int(moved), transcendentals=0),
    )(*inputs)


def load_params(move, pieces, rows, target):
    mine = lax.axis_index("dp")
    step_rows = pieces[0].shape[0] // 4
    width = target.shape[1] // 8
    copies = []
    for step in range(4):
        for side in range(2):
            owner = mine ^ (2 * step + side)
            copies.append(
                move.start(
                    pieces[side].at[pl.ds(step * step_rows + rows, PARAM_ROWS), pl.ds(0, width)],
                    target.at[:, pl.ds(pl.multiple_of(owner * width, width), width)],
                )
            )
    return copies


def attention_group(batches, weight, params, first_head, heads):
    count, width = batches[0][0].shape
    side = heads * HEAD
    pieces = len(weight)
    total = len(batches)
    tile = count // 4
    opening = params is None
    own_rows = width // 8 if pieces == 2 else width

    def body(*refs):
        each = 2 if opening else 3
        inputs = [refs[each * i : each * (i + 1)] for i in range(total)]
        w_refs = refs[each * total : each * total + pieces]
        at = each * total + pieces
        if not opening:
            p_ref = refs[at]
            at += 1
        outputs = []
        for _, _, _, keep in batches:
            outputs.append(refs[at : at + (6 if keep else 1)])
            at += 6 if keep else 1
        if opening:
            normed_outs = refs[at : at + total]
            col_outs = refs[at + total : at + 2 * total]
            z_out, p_out = refs[at + 2 * total : at + 2 * total + 2]
            at += 2 * total + 2
        params_v, w_v, *held = refs[at:-1]
        if opening:
            z_v, *held = held
        move = Mover(refs[-1])
        if not opening:
            loads = [move.start(p_ref, params_v)]
        else:
            loads = load_params(move, w_refs, own_rows, params_v)
        scratch, batch_loads = [], []
        for index, (_, _, _, keep) in enumerate(batches):
            scratch.append(held[: 9 if keep else 7])
            held = held[9 if keep else 7 :]
            normed_v, col_v, row_v = scratch[index][:3]
            batch_loads.append(move.start(inputs[index][0], normed_v))
            if index == 0:
                w_loads = load_rows(move, w_refs, w_v, rows=own_rows)
            ids = [move.start(inputs[index][1], row_v)]
            if not opening:
                ids.append(move.start(inputs[index][2], col_v))
            scratch[index] = (*scratch[index], ids)
        wait_all(loads)
        if opening:
            move.put(params_v, p_out)
        at = first_head * HEAD
        q_shift = params_v[3:4, at : at + side].astype(F32)
        v_shift = params_v[4:5, at : at + side].astype(F32)
        for index, (_, _, _, keep) in enumerate(batches):
            normed_v, col_v, row_v, q, k, v, o = scratch[index][:7]
            batch_loads[index].wait()
            if opening:
                gain = params_v[0:1, :].astype(F32)
                shift = params_v[2:3, :].astype(F32)
                for part in tiles_of(count, 208):
                    z, _ = normal_rows(normed_v[part, :].astype(F32))
                    normed_v[part, :] = (z * gain + shift).astype(BF16)
                    if keep:
                        z_v[part, :] = z.astype(BF16)
                move.put(normed_v, normed_outs[index])
                if keep:
                    move.put(z_v, z_out)
                wait_all(scratch[index][-1])
                top = lax.broadcasted_iota(jnp.int32, (16, count), 0) == 0
                spread = jnp.where(top, row_v[...].astype(F32), 0.0).astype(BF16)
                col_v[...] = dot_tn(spread, jnp.ones((16, 128), BF16))
                move.put(col_v, col_outs[index])
            if index == 0:
                wait_all(w_loads)
            for part in tiles_of(count, count):
                projected = dot_nn(normed_v[part, :], w_v[...])
                q[part, :] = (projected[:, :side] + q_shift).astype(BF16)
                k[part, :] = projected[:, side : 2 * side].astype(BF16)
                v[part, :] = (projected[:, 2 * side :] + v_shift).astype(BF16)
            if keep:
                q_out, k_out, v_out, o_out, e_out, l_out = outputs[index]
                e_all, inv = scratch[index][7:9]
                move.put(q, q_out)
                move.put(k, k_out)
                move.put(v, v_out)
            else:
                o_out = outputs[index][0]
            if not opening:
                wait_all(scratch[index][-1])
            row = row_v[...].astype(F32)
            for head in range(heads):
                lanes = pl.ds(head * HEAD, HEAD)
                key_rows = k[:, lanes]
                value_rows = v[:, lanes]
                wide = jnp.concatenate([value_rows, jnp.ones_like(value_rows)], axis=1)
                for part in tiles_of(count, tile):
                    scores = dot_nt(q[part, lanes], key_rows)
                    scores = jnp.where(col_v[part, 0:1] == row, scores, -1e30)
                    top = jnp.max(scores, axis=1, keepdims=True)
                    e = jnp.exp2(scores * (SCALE * LOG2E) - top * (SCALE * LOG2E)).astype(BF16)
                    if keep:
                        e_all[head, part, :] = e
                    both = dot_nn(e, wide)
                    inverse = 1.0 / both[:, HEAD:]
                    if keep:
                        inv[part, lanes] = inverse
                    o[part, lanes] = (both[:, :HEAD] * inverse).astype(BF16)
                if keep:
                    move.put(e_all.at[head], e_out.at[head])
            move.put(o, o_out)
            if keep:
                move.put(inv, l_out)
        move.finish()

    buf = pltpu.VMEM((count, side), BF16)
    scratch = [pltpu.VMEM((PARAM_ROWS, width), BF16), pltpu.VMEM((width, 3 * side), BF16)]
    scratch += [pltpu.VMEM((count, width), BF16)] if opening else []
    outs, inputs = [], []
    for normed, ids_col, ids_row, keep in batches:
        inputs += [normed, ids_row] if opening else [normed, ids_row, ids_col]
        scratch += [
            pltpu.VMEM((count, width), BF16), pltpu.VMEM((count, 128), F32),
            pltpu.VMEM(ids_row.shape, jnp.int32), buf, buf, buf, buf,
        ]
        outs += [sds((count, side))]
        if keep:
            scratch += [pltpu.VMEM((heads, count, count), BF16), pltpu.VMEM((count, side), F32)]
            outs += [sds((count, side))] * 3 + [sds((heads, count, count)), sds((count, side), F32)]
    if opening:
        outs += [sds((count, width))] * total + [sds((count, 128), F32)] * total
        outs += [sds((count, width)), sds((PARAM_ROWS, width))]
    flops = total * (2 * count * width * 3 * side + 8 * heads * count * count * HEAD)
    result = kernel_call(
        body, f"attention_{'_'.join('stash' if b[3] else 'fwd' for b in batches)}_{first_head}",
        (*inputs, *weight, *([] if opening else [params])),
        [ANY] * ((2 if opening else 3) * total + pieces + (0 if opening else 1)), outs, scratch,
        19 + total * (5 + 5 + heads), flops,
    )
    split = []
    for _, _, _, keep in batches:
        split.append(result[: 6 if keep else 1])
        result = result[6 if keep else 1 :]
    return split, result


def gelu_parts(hidden):
    square = hidden * hidden
    bend = jnp.tanh(GELU_C * hidden * (1.0 + GELU_A * square))
    half = 0.5 * (1.0 + bend)
    slope = half + 0.5 * hidden * (1.0 - bend * bend) * (GELU_C * (1.0 + 3.0 * GELU_A * square))
    return hidden * half, slope


def mlp_fwd(latents, mixed, weight, last, params, ids_col, cuts):
    count, width = latents.shape
    split = len(mixed)
    tile = count // 4

    def body(*refs):
        x_ref = refs[0]
        m_refs = refs[1 : 1 + split]
        w_ref, l_ref = refs[1 + split : 3 + split]
        p_ref, col_ref = refs[1 + split + 2 : 3 + split + 2]
        y_outs = refs[3 + split + 2 : 3 + split + 2 + len(cuts)]
        x, mixed_v, w, w_last, p, col, rest, n, y, sems = refs[3 + split + 2 + len(cuts) :]
        move = Mover(sems)
        loads = [move.start(p_ref, p), move.start(x_ref, x)]
        loads += load_side_by_side(move, m_refs, mixed_v)
        loads.append(move.start(w_ref, w.at[0]))
        load_next = [move.start(l_ref.at[0], w.at[1])]
        load_last = [move.start(l_ref.at[1], w_last), move.start(col_ref, col)]
        wait_all(loads)
        rows = [p[i : i + 1, :].astype(F32) for i in range(9)]
        for part in tiles_of(count, tile):
            attended = x[part, :].astype(F32) + dot_nn(mixed_v[part, :], w[0]) + rows[5]
            rest[part, :] = attended
            z, _ = normal_rows(attended)
            n[part, :] = (z * rows[1] + rows[6]).astype(BF16)
        wait_all(load_next)
        for index, part in enumerate(tiles_of(count, tile)):
            hidden = dot_nn(n[part, :], w[1]) + rows[7]
            active = gelu_parts(hidden)[0].astype(BF16)
            if index == 0:
                wait_all(load_last)
            result = rest[part, :] + dot_nn(active, w_last[...]) + rows[8]
            y[part, :] = jnp.where(col[part, 0:1] < 3, result, 0.0).astype(BF16)
        place = 0
        for out in y_outs:
            move.put(y.at[pl.ds(place, out.shape[0])], out)
            place += out.shape[0]
        move.finish()

    buf = pltpu.VMEM((count, width), BF16)
    return kernel_call(
        body, "mlp_fwd", (latents, *mixed, weight, last, params, ids_col),
        [ANY] * (3 + split + 2),
        [sds((rows, width)) for rows in cuts],
        [buf, buf, pltpu.VMEM((2, width, width), BF16), pltpu.VMEM((width, width), BF16),
         pltpu.VMEM(params.shape, BF16), pltpu.VMEM(ids_col.shape, F32),
         pltpu.VMEM((count, width), F32), buf, buf],
        3 + split + 24 + len(cuts), 6 * count * width * width,
    )


def middle_stash(latents, arrived, mixed, weight, last, params, ids_col, sides):
    count, width = latents.shape
    split = len(mixed)
    tile = count // 4
    wide = width // 4

    def body(*refs):
        g_refs, refs = refs[: len(arrived)], refs[len(arrived) - 1 :]
        x_ref = refs[1]
        m_refs = refs[2 : 2 + split]
        w_ref, l_ref = refs[2 + split : 4 + split]
        p_ref, col_ref, d_out, m_out, t_out = refs[2 + split + 2 : 7 + split + 2]
        grads = refs[7 + split + 2 : 7 + split + 2 + sides]
        (x, cot, mixed_v, w, w_last, p, col, n, z_v, r_v, act, slope_v, dhid, datt, dattn, dmix,
         terms, out_terms, sums, extra, sems) = refs[7 + split + 2 + sides :]
        move = Mover(sems)
        loads = [move.start(p_ref, p), move.start(x_ref, x)]
        loads += load_side_by_side(move, m_refs, mixed_v)
        loads.append(move.start(w_ref, w.at[0]))
        load_next = [move.start(l_ref.at[0], w.at[1])]
        load_back, place = [move.start(col_ref, col)], 0
        for ref in g_refs:
            load_back.append(move.start(ref, cot.at[pl.ds(place, ref.shape[0])]))
            place += ref.shape[0]
        load_last = [move.start(l_ref.at[1], w_last)]
        wait_all(loads)
        rows = [p[i : i + 1, :].astype(F32) for i in range(9)]
        for index, part in enumerate(tiles_of(count, tile)):
            attended = x[part, :].astype(F32) + dot_nn(mixed_v[part, :], w[0]) + rows[5]
            z, root = normal_rows(attended)
            z_v[part, :] = z.astype(BF16)
            r_v[part, :] = jnp.broadcast_to(root, (tile, 128))
            n[part, :] = (z * rows[1] + rows[6]).astype(BF16)
            if index == 0:
                wait_all(load_next)
            hidden = dot_nn(n[part, :], w[1]) + rows[7]
            active, slope = gelu_parts(hidden)
            act[part, :] = active.astype(BF16)
            slope_v[part, :] = slope.astype(BF16)
        wait_all(load_back)
        cot[...] = jnp.where(col[:, 0:1] < 3, cot[...].astype(F32), 0.0).astype(BF16)
        wait_all(load_last)
        totals = [jnp.zeros((1, width), F32) for _ in range(5)]
        for index, part in enumerate(tiles_of(count, tile)):
            dactive = dot_nt(cot[part, :], w_last[...])
            held = (slope_v[part, :].astype(F32) * dactive).astype(BF16)
            dhid[part, :] = held
            totals[3] += column_sum(held.astype(F32))
            totals[4] += column_sum(cot[part, :].astype(F32))
            block = pl.ds(index * wide, wide)
            terms[block, width:] = dot_tn(act[:, block], cot[...]).astype(BF16)
        move.put(terms.at[:, pl.ds(width, width)], t_out.at[:, pl.ds(width, width)])
        for index, part in enumerate(tiles_of(count, tile)):
            dnormed = dot_nt(dhid[part, :], w[1])
            z = z_v[part, :].astype(F32)
            totals[0] += column_sum(dnormed * z)
            totals[1] += column_sum(dnormed)
            dz = dnormed * rows[1]
            inner = dz - jnp.mean(dz, axis=-1, keepdims=True)
            inner = inner - z * jnp.mean(dz * z, axis=-1, keepdims=True)
            dattended = cot[part, :].astype(F32) + r_v[part, 0:1] * inner
            datt[part, :] = dattended
            held = dattended.astype(BF16)
            dattn[part, :] = held
            totals[2] += column_sum(held.astype(F32))
            block = pl.ds(index * wide, wide)
            terms[block, :width] = dot_tn(n[:, block], dhid[...]).astype(BF16)
            dmix[part, :] = dot_nt(held, w[0]).astype(BF16)
            move.put(datt.at[part], d_out.at[part])
            move.put(dmix.at[part], m_out.at[part])
        move.put(terms.at[:, pl.ds(0, width)], t_out.at[:, pl.ds(0, width)])
        for index in range(5):
            sums[index : index + 1, :] = totals[index]
        sums[5:PARAM_ROWS, :] = jnp.zeros((PARAM_ROWS - 5, width), F32)
        extra[...] = sums[...].astype(BF16)
        store_terms(move, out_terms, mixed_v, dattn, grads, extra)
        move.finish()

    buf = pltpu.VMEM((count, width), BF16)
    square = pltpu.VMEM((width, width), BF16)
    return kernel_call(
        body, "middle_stash", (*arrived, latents, *mixed, weight, last, params, ids_col),
        [ANY] * (3 + len(arrived) + split + 2),
        [sds((count, width), F32), sds((count, width)), sds((width, 2 * width))]
        + term_shapes(width, width, sides),
        [buf, buf, buf, pltpu.VMEM((2, width, width), BF16), square, pltpu.VMEM(params.shape, BF16),
         pltpu.VMEM(ids_col.shape, F32), buf, buf, pltpu.VMEM((count, 128), F32), buf, buf, buf,
         pltpu.VMEM((count, width), F32), buf, buf, pltpu.VMEM((width, 2 * width), BF16), square,
         pltpu.VMEM((PARAM_ROWS, width), F32), pltpu.VMEM((PARAM_ROWS, width), BF16)],
        3 + len(arrived) + split + 24 + 8 + 2 + 2 * lax.axis_size("dp"), 16 * count * width * width,
    )


def attention_backward(saved, dmixed, z_rows, first_head, heads, sides):
    count, width = z_rows.shape
    side = heads * HEAD
    tile = count // 2
    cuts, at = [], 0
    for index, arrays in enumerate(saved):
        own = arrays[0].shape[1] // HEAD
        low, high = max(first_head, at), min(first_head + heads, at + own)
        if low < high:
            cuts.append((index, low - at, low - first_head, high - low))
        at += own
    saved = [saved[cut[0]] for cut in cuts]
    groups = len(saved)

    def body(*refs):
        inputs = [refs[6 * i : 6 * i + 6] for i in range(groups)]
        m_ref, n_ref, d_out = refs[6 * groups : 6 * groups + 3]
        grads = refs[6 * groups + 3 : 6 * groups + 3 + sides]
        q, k, v, o, e, inv, dmix, n, dqkv, dscore, terms, sums, extra, sems = refs[
            6 * groups + 3 + sides :
        ]
        move = Mover(sems)
        load_m = move.start(m_ref.at[:, pl.ds(first_head * HEAD, side)], dmix)
        small, large = [], []
        for (q_ref, k_ref, v_ref, o_ref, e_ref, l_ref), cut in zip(inputs, cuts, strict=True):
            _, low, place, own = cut
            for head in range(own):
                source = pl.ds((low + head) * HEAD, HEAD)
                lanes = pl.ds((place + head) * HEAD, HEAD)
                small.append(
                    [
                        move.start(ref.at[:, source], target.at[:, lanes])
                        for ref, target in ((l_ref, inv), (o_ref, o), (v_ref, v))
                    ]
                )
                large.append(move.start(e_ref.at[low + head], e.at[place + head]))
                small[-1] += [
                    move.start(ref.at[:, source], target.at[:, lanes])
                    for ref, target in ((k_ref, k), (q_ref, q))
                ]
        load_n = move.start(n_ref, n)
        load_m.wait()
        for head in range(heads):
            lanes = pl.ds(head * HEAD, HEAD)
            wait_all(small[head])
            scaled = (dmix[:, lanes].astype(F32) * inv[:, lanes]).astype(BF16)
            row_sum = jnp.sum(scaled.astype(F32) * o[:, lanes].astype(F32), axis=1, keepdims=True)
            value_rows = v[:, lanes]
            head_keys = k[:, lanes]
            large[head].wait()
            for start in range(0, count, tile):
                part = pl.ds(start, tile)
                dprobs = dot_nt(scaled[start : start + tile], value_rows)
                held = e[head, part, :].astype(F32) * (dprobs - row_sum[start : start + tile])
                held = held.astype(BF16)
                dscore[part, :] = held
                dqkv[part, lanes] = (dot_nn(held, head_keys) * SCALE).astype(BF16)
            dqkv[:, pl.ds(side + head * HEAD, HEAD)] = (
                dot_tn(dscore[...], q[:, lanes]) * SCALE
            ).astype(BF16)
            dqkv[:, pl.ds(2 * side + head * HEAD, HEAD)] = dot_tn(e[head], scaled).astype(BF16)
        move.put(dqkv, d_out)
        sums[0:1, :] = column_sum(dqkv[...].astype(F32))
        sums[1:PARAM_ROWS, :] = jnp.zeros((PARAM_ROWS - 1, 3 * side), F32)
        extra[...] = sums[...].astype(BF16)
        load_n.wait()
        store_terms(move, terms, n, dqkv, grads, extra)
        move.finish()

    buf = pltpu.VMEM((count, side), BF16)
    return kernel_call(
        body, f"attention_backward_{first_head}",
        (*[array for group in saved for array in group], dmixed, z_rows),
        [ANY] * (6 * groups + 2),
        [sds((count, 3 * side))] + term_shapes(width, 3 * side, sides),
        [buf, buf, buf, buf, pltpu.VMEM((heads, count, count), BF16), pltpu.VMEM((count, side), F32),
         buf, pltpu.VMEM((count, width), BF16), pltpu.VMEM((count, 3 * side), BF16),
         pltpu.VMEM((count, count), BF16), pltpu.VMEM((width, 3 * side), BF16),
         pltpu.VMEM((PARAM_ROWS, 3 * side), F32), pltpu.VMEM((PARAM_ROWS, 3 * side), BF16)],
        3 + 6 * heads + 2 * lax.axis_size("dp"), 2 * count * width * 3 * side + 16 * heads * count * count * HEAD,
    )


def input_backward(latents, dattended, parts, weights, params, results):
    count, width = latents.shape
    pieces = len(weights[0])
    groups = len(parts)
    total = len(weights)
    tile = count // 4

    def body(*refs):
        x_ref, d_ref = refs[:2]
        g_refs = refs[2 : 2 + groups]
        at = 2 + groups
        w_refs = [refs[at + i * pieces : at + (i + 1) * pieces] for i in range(total)]
        at += total * pieces
        r_refs = refs[at : at + len(results)]
        at += len(results)
        p_ref, y_out, r_out, x, datt, dqkv, w, acc, y, r_v, p, sems = refs[at:]
        move = Mover(sems)
        loads = []
        for kind in range(3):
            own_loads = []
            place = 0
            for ref in g_refs:
                own = ref.shape[1] // 3
                own_loads.append(
                    move.start(ref.at[:, pl.ds(kind * own, own)], dqkv.at[kind, :, pl.ds(place, own)])
                )
                place += own
            place = 0
            for ref in w_refs:
                own = ref[0].shape[1] // 3
                own_loads += load_rows(
                    move, ref, w.at[kind, :, pl.ds(place, own)], pl.ds(kind * own, own), width // 8
                )
                place += own
            loads.append(own_loads)
        late = [move.start(x_ref, x), move.start(d_ref, datt), move.start(p_ref, p)]
        back, place = [], 0
        for ref in r_refs:
            back.append(move.start(ref, r_v.at[pl.ds(place, ref.shape[0])]))
            place += ref.shape[0]
        for kind in range(2):
            wait_all(loads[kind])
            for part in tiles_of(count, tile):
                dnormed = dot_nt(dqkv[kind, part, :], w[kind])
                acc[part, :] = dnormed if kind == 0 else acc[part, :] + dnormed
        wait_all(loads[2] + late)
        gain = p[0:1, :].astype(F32)
        for part in tiles_of(count, tile):
            dnormed = acc[part, :] + dot_nt(dqkv[2, part, :], w[2])
            z, root = normal_rows(x[part, :].astype(F32))
            dz = dnormed * gain
            inner = dz - jnp.mean(dz, axis=-1, keepdims=True)
            inner = inner - z * jnp.mean(dz * z, axis=-1, keepdims=True)
            y[part, :] = (datt[part, :] + root * inner).astype(BF16)
            move.put(y.at[part], y_out.at[part])
        wait_all(back)
        move.put(r_v, r_out)
        move.finish()

    buf = pltpu.VMEM((count, width), BF16)
    return kernel_call(
        body, "input_backward",
        (latents, dattended, *parts, *[piece for weight in weights for piece in weight], *results,
         params),
        [ANY] * (3 + groups + total * pieces + len(results)),
        [sds((count, width)), sds((count, width))],
        [buf, pltpu.VMEM((count, width), F32), pltpu.VMEM((3, count, width), BF16),
         pltpu.VMEM((3, width, width), BF16), pltpu.VMEM((count, width), F32), buf, buf,
         pltpu.VMEM(params.shape, BF16)],
        3 + 3 * groups + 24 * total + len(results) + 5, 6 * count * width * width,
    )


def swapped(value, axis, flip):
    count = lax.axis_size(axis)
    return lax.ppermute(value, axis, [(source, source ^ flip) for source in range(count)])


def shifted(value, axis, steps):
    count = lax.axis_size(axis)
    pairs = [(source, (source + steps) % count) for source in range(count)]
    return lax.ppermute(value, axis, pairs)


def after(value, *others):
    return lax.optimization_barrier((value, *others))[0]


def all_after(values, *markers):
    return lax.optimization_barrier((*values, *markers))[: len(values)]


def send_rows(shard):
    if lax.axis_size("dp") != 8:
        return (lax.all_gather(shard, "dp", axis=0, tiled=True),)
    return tuple(swapped(shard, "dp", flip) for flip in (2, 4, 6))


def join_rows(shard, arrived):
    if len(arrived) == 1:
        return arrived
    side = jnp.concatenate([shard, *arrived], axis=0)
    return side, swapped(side, "dp", 1)


def added(*values):
    total = values[0].astype(F32)
    for value in values[1:]:
        total = total + value.astype(F32)
    return total


def sum_stages(pieces):
    if lax.axis_size("dp") != 8:
        shard = lax.psum_scatter(pieces[0], "dp", scatter_dimension=0, tiled=True)
        shard = lax.psum(shard, "pipe")
        (shard,) = yield (), (shard,)
        yield None, shard.astype(F32)
        return
    mine, theirs = pieces
    (other,) = yield (theirs,), (swapped(theirs, "dp", 1),)
    rows = mine.shape[0] // 4
    pair = []
    for step in range(4):
        part = slice(step * rows, (step + 1) * rows)
        pair.append(added(mine[part], other[part]).astype(BF16))
    arrived = yield pair, tuple(swapped(pair[step], "dp", 2 * step) for step in (1, 2, 3))
    kept = rows - PARAM_ROWS // 2
    shard = added(pair[0][:kept], *[value[:kept] for value in arrived]).astype(BF16)
    flip = 1
    while flip < lax.axis_size("pipe"):
        (other,) = yield (shard,), (swapped(shard, "pipe", flip),)
        flip *= 2
        shard = added(shard, other)
        if flip < lax.axis_size("pipe"):
            shard = shard.astype(BF16)
    yield None, shard


def line_stages(shard):
    count = lax.axis_size("pipe")
    if count != 4:
        yield None, lax.psum(shard, "pipe").astype(F32)
        return
    (other,) = yield (shard,), (lax.ppermute(shard, "pipe", [(0, 1), (3, 2)]),)
    shard = added(shard, other).astype(BF16)
    (other,) = yield (shard,), (lax.ppermute(shard, "pipe", [(1, 2), (2, 1)]),)
    shard = added(shard, other).astype(BF16)
    (other,) = yield (shard,), (lax.ppermute(shard, "pipe", [(1, 0), (2, 3)]),)
    place = lax.axis_index("pipe")
    yield None, jnp.where((place == 0) | (place == 3), other, shard).astype(F32)


class Chunk:
    def __init__(self, terms, stages=sum_stages):
        self.stages = stages(terms)
        self.sent, self.result = next(self.stages)

    def step(self, *markers):
        if self.sent is None:
            return ()
        arrived = all_after(self.result, *markers) if markers else self.result
        self.sent, self.result = self.stages.send(arrived)
        return (self.result,) if self.sent is None else self.sent

    def finish(self):
        while self.sent is not None:
            self.step()
        return self.result


def local(
    fwd_latents,
    fwd_segments,
    stash_latents,
    stash_segments,
    upstream_grad,
    qkv_weight,
    out_weight,
    mlp_weight,
    norm_gain,
    biases,
):
    fwd_x, stash_x = fwd_latents[0], stash_latents[0]
    count, width = fwd_x.shape
    pieces = 2 if lax.axis_size("dp") == 8 else 1
    fwd_row, stash_row = fwd_segments, stash_segments
    fwd_col = stash_col = None
    own = norm_gain.shape[1]
    small = jnp.concatenate(
        [norm_gain, biases, jnp.zeros((PARAM_ROWS - 9, own), norm_gain.dtype)], axis=0
    )

    def qkv_shard(first, heads):
        cut = qkv_weight[:, :, first * HEAD : (first + heads) * HEAD]
        return jnp.concatenate([cut[0], cut[1], cut[2]], axis=1)

    first_shard = qkv_shard(*FORWARD_GROUPS[0])
    if pieces == 2:
        small = jnp.pad(small, ((0, 0), (0, first_shard.shape[1] - own)))
        first_shard = jnp.concatenate([first_shard, small], axis=0)
    qkv_shards = [first_shard] + [qkv_shard(*group) for group in FORWARD_GROUPS[1:]]
    flights = []
    for shard in qkv_shards:
        if flights:
            shard = after(shard, *flights[-1])
        flights.append(send_rows(shard))
    middle = jnp.concatenate([out_weight, mlp_weight[0]], axis=1)
    middle = (lax.all_gather(after(middle, *flights[0]), "dp", axis=0, tiled=True),)
    middle = lax.all_gather(after(out_weight, first_shard), "dp", axis=0, tiled=True)
    last = lax.all_gather(after(mlp_weight, first_shard), "dp", axis=1, tiled=True)
    gathered = [join_rows(qkv_shards[0], flights[0])]
    if pieces == 1:
        params = lax.all_gather(small, "dp", axis=1, tiled=True)
    else:
        params = None
    half = count // 32 * 16
    upstream = upstream_grad[0]
    cotangent = [shifted(upstream[:half], "pipe", -1), shifted(upstream[half:], "pipe", -1)]

    saved, fwd_mixed = [], []
    normed = (stash_x, fwd_x)
    if params is not None:
        stash_col, fwd_col = (
            jnp.broadcast_to(row[0].astype(F32)[:, None], (count, 128)) for row in (stash_row, fwd_row)
        )
        plain = [normal_rows(rows.astype(F32))[0] for rows in normed]
        z_rows = plain[0].astype(BF16)
        normed = tuple(
            (rows * params[0:1].astype(F32) + params[2:3].astype(F32)).astype(BF16)
            for rows in plain
        )
    for index, (first, heads) in enumerate(FORWARD_GROUPS):
        (kept, plain), extra = attention_group(
            [(normed[0], stash_col, stash_row, True), (normed[1], fwd_col, fwd_row, False)],
            gathered[index], params, first, heads,
        )
        if extra:
            normed, (stash_col, fwd_col, z_rows, params) = tuple(extra[:2]), extra[2:]
        saved.append(kept)
        fwd_mixed.append(plain[0])
        here = ()
        if index:
            here = all_after((cotangent[index - 1],), plain[0])
            cotangent[index - 1] = here[0]
        if index + 1 < len(FORWARD_GROUPS):
            arrived = all_after(flights[index + 1], plain[0], *here)
            gathered.append(join_rows(qkv_shards[index + 1], arrived))
    stash_mixed = [group[3] for group in saved]
    dattended, dmixed, mlp_terms, *terms = middle_stash(
        stash_x, cotangent, stash_mixed, middle, last, params, stash_col, pieces
    )
    mlp_part = lax.psum_scatter(mlp_terms, "dp", scatter_dimension=0, tiled=True)
    running = [Chunk(terms)]

    def advance(marker):
        return [value for chunk in running for value in chunk.step(marker)]

    def begin(terms, sent):
        running.append(Chunk([*terms[:-1], after(terms[-1], *sent)]))
        return running[-1].step()

    result = mlp_fwd(
        after(fwd_x, dmixed), fwd_mixed, middle, last, params, fwd_col, (half, count - half)
    )
    latents = [shifted(rows, "pipe", 1) for rows in result]
    sent = advance(result[0])
    dprojected = []
    for index, (first, heads) in enumerate(BACKWARD_GROUPS):
        part, *terms = attention_backward(
            saved, after(dmixed, *sent), z_rows, first, heads, pieces
        )
        dprojected.append(part)
        sent = advance(part)
        if index < 2:
            (latents[index],) = all_after((latents[index],), part)
            sent.append(latents[index])
        if index == 1:
            (mlp_part,) = all_after((mlp_part,), part)
            mlp_total = lax.psum(mlp_part, "pipe")
            sent.append(mlp_part)
        sent += begin(terms, sent)
        dmixed = after(dmixed, part)
    input_grad, latents = input_backward(
        after(stash_x, *sent), dattended, dprojected, gathered, params, latents
    )
    newest, *older = running[::-1]
    sent = newest.step(input_grad)
    for chunk in older:
        sent = (*sent, *chunk.step(input_grad, *sent))
    sent = newest.step(*sent)
    (mlp_total,) = all_after((mlp_total,), input_grad, *sent)
    mlp_total = mlp_total.astype(F32)
    out_total, *qkv_totals = [chunk.finish() for chunk in running]

    out_total, norm_gain, biases = all_after((out_total, norm_gain, biases), *sent)
    rows = qkv_weight.shape[1]
    gain = norm_gain[0].astype(F32)[:, None]
    shift = biases[0].astype(F32)[:, None]
    grads, sums, gain_first, shift_first = [], [], 0.0, 0.0
    for kind in range(3):
        cut = [
            total[:, kind * total.shape[1] // 3 : (kind + 1) * total.shape[1] // 3]
            for total in qkv_totals
        ]
        cut = jnp.concatenate(cut, axis=1)
        weight = qkv_weight[kind].astype(F32)
        grads.append(gain * cut[:rows] + shift * cut[rows : rows + 1])
        sums.append(cut[rows : rows + 1])
        gain_first += jnp.sum(weight * cut[:rows], axis=1)
        shift_first += jnp.sum(weight * cut[rows : rows + 1], axis=1)
    place = lax.axis_index("dp") * rows

    def own_part(row):
        return lax.dynamic_slice_in_dim(row, place, rows, axis=row.ndim - 1)

    late = own_part(out_total[rows : rows + 5])
    gain_grad = jnp.stack([gain_first, late[0]])
    bias_grad = jnp.stack(
        [shift_first, own_part(sums[0][0]), own_part(sums[2][0]), late[2], late[1], late[3], late[4]]
    )
    return (
        latents[None],
        input_grad[None],
        jnp.stack(grads),
        out_total[:rows],
        jnp.stack([mlp_total[:, :width], mlp_total[:, width:]]),
        gain_grad,
        bias_grad,
        late[1],
    )


def solution(mesh):
    in_specs = (
        P("pipe", "dp", None),
        P("pipe", "dp"),
        P("pipe", "dp", None),
        P("pipe", "dp"),
        P("pipe", "dp", None),
        P(None, "dp", None),
        P("dp", None),
        P(None, "dp", None),
        P(None, "dp"),
        P(None, "dp"),
    )
    out_specs = (
        P("pipe", "dp", None),
        P("pipe", "dp", None),
        P(None, "dp", None),
        P("dp", None),
        P(None, "dp", None),
        P(None, "dp"),
        P(None, "dp"),
        P("dp"),
    )
    return jax.shard_map(local, mesh=mesh, in_specs=in_specs, out_specs=out_specs, check_vma=False)
```
